256 devices in a mesh: cells: 256 (over y, x, z, core).
Axes of the slice: x: 4, y: 4, z: 8, core: 2. Of those that a mesh axis runs over, the one named last changes fastest.
Arguments:
- probes: bfloat16 [16, 64, 262144], P(None, None, 'cells'), may hold values from -6 to 6
- area: float32 [262144], P('cells'), may hold values from 1 to 30, as said below
- settle: float32 [16, 262144], P(None, 'cells'), may hold values from 0.05 to 0.5
- courant: float32 [3, 16, 262144], P(None, None, 'cells'), may hold values from 0.02 to 0.3
- orient: int32 [3, 16, 262144], P(None, None, 'cells'), may hold values from 0 to 1
- local_slot: int32 [3, 262144], P(None, 'cells'), may hold values from 0 to 1535, as said below
- send_rows: int32 [131072], P('cells'), may hold values from 0 to 1023, as said below
Outputs:
- basis: float32 [16, 64, 262144], P(None, None, 'cells')
- factor: float32 [64, 64], replicated
The draws below stay inside these ranges and needn't reach their ends.
Inputs may be any that keep to these rules, and one draw needn't show every extreme that they name: `local_slot`: slot of the neighbour across face j of cell c in its device's table; a face whose slot is the cell itself is a closed boundary. The first device references no slot of the previous side and the last none of the next side. `send_rows`: entries 2 * 256 * d to 2 * 256 * (d + 1) - 1 are own-cell indices of device d: first the rows for device d - 1, then the rows for device d + 1; entries that no receiver's slot refers to are 0. `area`: areas are positive.
All inputs are finite; a program needn't handle non-finite values.
Results may differ from the reference program's by a relative error of at most 0.0014.
The reference program's roundings to bfloat16 on the way count: a program that leaves them out, or rounds other values in their place, can miss the bound.
Values may be sent and summed in bfloat16 or wider, within the bound.
A program may use at most 128 MiB of HBM per device.

```python
import math
import jax
import jax.numpy as jnp
from jax import lax

CELL_DEV = 1024
LAYERS = 16
PROBES = 64
HALO = 256
CELLS = 262144
ROWS = 4194304
N_CELLS = 256


def ghost_counts(key):
    base = jax.random.randint(jax.random.fold_in(key, 11), (N_CELLS, 2), HALO // 4, HALO + 1)
    chosen = jax.random.randint(jax.random.fold_in(key, 12), (), 1, N_CELLS - 1)
    devices = jnp.arange(N_CELLS)
    base = jnp.where((devices == chosen)[:, None], HALO, base)
    left = jnp.where(devices == 0, 0, base[:, 0])
    right = jnp.where(devices == N_CELLS - 1, 0, base[:, 1])
    return (left, right, chosen)


def draw_local_slot(key, part):
    left, right, chosen = ghost_counts(key)
    own = jax.random.randint(jax.random.fold_in(key, 21), (3, N_CELLS, CELL_DEV), 0, CELL_DEV)
    cell = jnp.arange(CELL_DEV)
    mirror = CELL_DEV - 1 - cell
    first = jnp.where(cell[None, :] < left[:, None], CELL_DEV + cell[None, :], own[0])
    second = jnp.where(mirror[None, :] < right[:, None], CELL_DEV + HALO + mirror[None, :], own[1])
    slots = jnp.stack([first, second, own[2]])
    return slots.reshape(3, N_CELLS * CELL_DEV).astype(jnp.int32)


def draw_send_rows(key, part):
    left, right, chosen = ghost_counts(key)
    rows = jax.random.randint(jax.random.fold_in(key, 31), (N_CELLS, 2 * HALO), 0, CELL_DEV)
    slot = jnp.arange(2 * HALO)
    zero = jnp.zeros((1,), left.dtype)
    prev_right = jnp.concatenate([zero, right[:-1]])
    next_left = jnp.concatenate([left[1:], zero])
    live = jnp.where(slot[None, :] < HALO, slot[None, :] < prev_right[:, None], slot[None, :] - HALO < next_left[:, None])
    rows = jnp.where(live, rows, 0)
    devices = jnp.arange(N_CELLS)
    rows = jnp.where((devices == chosen)[:, None] & (slot == HALO)[None, :], CELL_DEV - 1, rows)
    return rows.reshape(-1).astype(jnp.int32)


def draw_area(key, part):
    total = N_CELLS * CELL_DEV
    place = jnp.arange(total).astype(jnp.float32) / jnp.float32(total - 1)
    ramp = jnp.exp(place * math.log(3.0))
    rough = jnp.exp(jax.random.uniform(jax.random.fold_in(key, 41), (total,), jnp.float32, 0.0, math.log(10.0)))
    return (ramp * rough).astype(jnp.float32)


def set_ends(values, key, low, largest):
    spot = [jax.random.randint(jax.random.fold_in(key, axis), (), 0, length) for axis, length in enumerate(values.shape)]
    widest = values.shape.index(max(values.shape))
    beside = spot[:widest] + [(spot[widest] + 1) % values.shape[widest]] + spot[widest + 1:]
    return values.at[tuple(spot)].set(low).at[tuple(beside)].set(largest)


def levels(rng, extent, shards, low, high):
    loudness = 1.0
    for dim, shards_of in shards:
        draws = jax.random.uniform(jax.random.fold_in(jax.random.fold_in(rng, 6), dim), (shards_of,), jnp.float32, low / len(shards), high / len(shards))
        loudness = loudness * jnp.repeat(jnp.exp(draws), extent[dim] // shards_of).reshape((-1,) + (1,) * (len(extent) - 1 - dim))
    return loudness


def noise(rng, dims, deviation, most, pieces=(), kind=jnp.bfloat16):
    level = levels(rng, dims, pieces, -0.22, 0.18) if pieces else 1.0
    result = jax.random.normal(rng, dims, jnp.float32) * deviation * level
    return jnp.minimum(jnp.maximum(result, -most), most).astype(kind)


def setup_inputs(seed: int = 0) -> dict:
    key_list = jax.random.split(jax.random.key(seed), 8)
    return {
        "probes": noise(key_list[0], (LAYERS, PROBES, CELLS), 1.0, 6.0, ((2, 256),)),
        "area": draw_area(jax.random.fold_in(key_list[7], 71), 0),
        "settle": jnp.clip(jnp.exp(math.log(0.5) - 2.3025851 * jax.random.uniform(key_list[2], (LAYERS, CELLS), jnp.float32) ** levels(key_list[2], (LAYERS, CELLS), ((1, 256),), -0.2, 0.2)), 0.05, 0.5),
        "courant": jnp.clip(0.02 + 0.28 * jax.random.uniform(key_list[3], (3, LAYERS, CELLS), jnp.float32) ** levels(key_list[3], (3, LAYERS, CELLS), ((2, 256),), -0.2, 0.2), 0.02, 0.3),
        "orient": set_ends(jax.random.randint(key_list[4], (3, LAYERS, CELLS), 0, 2), jax.random.fold_in(key_list[4], 1), 0, 1).astype(jnp.int32),
        "local_slot": draw_local_slot(jax.random.fold_in(key_list[7], 71), 0),
        "send_rows": draw_send_rows(jax.random.fold_in(key_list[7], 71), 0),
    }


def upper_factor(gram):
    width = gram.shape[0]
    index = jnp.arange(width, dtype=jnp.int32)

    def column(step, carry):
        rest, upper = carry
        pivot = jnp.sqrt(lax.dynamic_index_in_dim(lax.dynamic_index_in_dim(rest, step, 0, keepdims=False), step, 0, keepdims=False))
        row_now = lax.dynamic_index_in_dim(rest, step, 0, keepdims=False) / pivot
        row_now = jnp.where(index >= step, row_now, jnp.zeros_like(row_now))
        rest = rest - row_now[:, None] * row_now[None, :]
        upper = lax.dynamic_update_index_in_dim(upper, row_now, step, 0)
        return (rest, upper)
    _, upper = lax.fori_loop(0, width, column, (gram, jnp.zeros_like(gram)))
    return upper

def upper_inverse(upper):
    width = upper.shape[0]
    identity = jnp.eye(width, dtype=upper.dtype)

    def row_step(turn, inverse):
        step = width - 1 - turn
        urow = lax.dynamic_index_in_dim(upper, step, 0, keepdims=False)
        pivot = lax.dynamic_index_in_dim(urow, step, 0, keepdims=False)
        known = jnp.dot(urow, inverse, precision=lax.Precision.HIGHEST)
        erow = lax.dynamic_index_in_dim(identity, step, 0, keepdims=False)
        return lax.dynamic_update_index_in_dim(inverse, (erow - known) / pivot, step, 0)
    return lax.fori_loop(0, width, row_step, jnp.zeros_like(upper))

def neighbours(local_slot, send_rows):
    send = send_rows.reshape(N_CELLS, 2 * HALO)
    owner = (jnp.arange(CELLS, dtype=jnp.int32) // CELL_DEV)[None, :]
    before = jnp.clip(owner - 1, 0, N_CELLS - 1)
    after = jnp.clip(owner + 1, 0, N_CELLS - 1)
    left_slot = jnp.clip(local_slot - CELL_DEV, 0, HALO - 1)
    right_slot = jnp.clip(local_slot - CELL_DEV - HALO, 0, HALO - 1)
    from_left = before * CELL_DEV + send[before, HALO + left_slot]
    from_right = after * CELL_DEV + send[after, right_slot]
    own = owner * CELL_DEV + local_slot
    return jnp.where(local_slot < CELL_DEV, own, jnp.where(local_slot < CELL_DEV + HALO, from_left, from_right)).astype(jnp.int32)

def layer_rows(layer, probes, area, settle, courant, orient, nb):
    lam = lax.dynamic_index_in_dim(probes, layer, 0, keepdims=False).astype(jnp.float32)
    lower = jnp.minimum(layer + 1, LAYERS - 1)
    below = lax.dynamic_index_in_dim(probes, lower, 0, keepdims=False).astype(jnp.float32)
    below = jnp.where(layer < LAYERS - 1, below, jnp.zeros_like(below))
    scaled = (lam / area[None, :]).astype(jnp.bfloat16)
    scaled = lax.optimization_barrier(scaled).astype(jnp.float32)
    rate = lax.dynamic_index_in_dim(settle, layer, 0, keepdims=False)
    mu = lam + rate[None, :] * (below - lam)
    for face in range(3):
        flux = lax.dynamic_index_in_dim(courant[face], layer, 0, keepdims=False)
        leaves = lax.dynamic_index_in_dim(orient[face], layer, 0, keepdims=False).astype(jnp.float32)
        other = jnp.take(scaled, nb[face], axis=1)
        mu = mu + (flux * leaves)[None, :] * (area[None, :] * other - lam)
    return jnp.sqrt(area)[None, :] * mu

def reference(probes, area, settle, courant, orient, local_slot, send_rows):
    nb = neighbours(local_slot, send_rows)
    layers = jnp.arange(LAYERS, dtype=jnp.int32)

    def accumulate(gram, layer):
        rows = layer_rows(layer, probes, area, settle, courant, orient, nb)
        return (gram + jnp.dot(rows, rows.T, precision=lax.Precision.HIGHEST), None)
    gram, _ = lax.scan(accumulate, jnp.zeros((PROBES, PROBES), jnp.float32), layers)
    upper = upper_factor(gram)
    inverse = upper_inverse(upper)
    scale = jnp.sqrt(jnp.float32(ROWS))

    def finish(layer):
        rows = layer_rows(layer, probes, area, settle, courant, orient, nb)
        return jnp.dot(inverse.T, rows, precision=lax.Precision.HIGHEST) * scale
    basis = lax.map(finish, layers)
    return (basis, upper / scale)
```

```python
import functools
import math

import jax
import jax.numpy as jnp
from jax import lax
from jax.experimental import pallas as pl
from jax.experimental.pallas import tpu as pltpu
from jax.sharding import PartitionSpec as P

MESH = pl.DeviceIdType.MESH
GROUP = 16
TILE = 256
NT = (((1,), (1,)), ((), ()))


def advect_kernel(
    devices, probes, area, settle, courant, orient, slots, sends, pairs_out, gram_out,
    v, outgoing, ghosts, total, pairs, parts, recv_a, recv_b, recv_c,
    halo_send, halo_recv, send_sem, recv_sem, store_sem,
):
    layers, cells = settle.shape
    width = probes.shape[0] // layers
    halo = ghosts.shape[2]
    chunks = probes.shape[0] // TILE
    others = devices // GROUP
    me = lax.axis_index("cells")
    left, right = lax.rem(me + devices - 1, devices), lax.rem(me + 1, devices)
    place = lax.rem(me, GROUP)
    base = me - place
    block = me // GROUP

    barrier = pltpu.get_barrier_semaphore()
    for side in (left, right):
        pl.semaphore_signal(barrier, inc=1, device_id=(side,), device_id_type=MESH)

    def greet(step, _):
        near = base + lax.rem(place + step, GROUP)
        far = lax.rem(block + step, others) * GROUP + place
        pl.semaphore_signal(barrier, inc=1, device_id=(near,), device_id_type=MESH)
        pl.semaphore_signal(barrier, inc=1, device_id=(far,), device_id_type=MESH)
        return 0

    lax.fori_loop(1, GROUP, greet, 0)

    one, zero = jnp.bfloat16(1), jnp.bfloat16(0)
    cell_area = area[...]
    inverse_area = 1.0 / cell_area
    pick = jnp.where(
        lax.broadcasted_iota(jnp.int32, (cells, 2 * halo), 0) == sends[...], one, zero
    )
    copies = []
    for chunk in range(chunks):
        rows = pl.ds(chunk * TILE, TILE)
        part = (probes[rows, :].astype(jnp.float32) * inverse_area).astype(jnp.bfloat16)
        v[rows, :] = part
        picked = jnp.dot(part, pick, preferred_element_type=jnp.float32).astype(jnp.bfloat16)
        outgoing[0, rows, :] = picked[:, :halo]
        outgoing[1, rows, :] = picked[:, halo:]
        if chunk == 0:
            pl.semaphore_wait(barrier, 2 * GROUP)
        for side, target in ((0, left), (1, right)):
            copy = pltpu.make_async_remote_copy(
                src_ref=outgoing.at[side, rows, :],
                dst_ref=ghosts.at[1 - side, rows, :],
                send_sem=halo_send.at[side, chunk],
                recv_sem=halo_recv.at[1 - side, chunk],
                device_id=(target,),
                device_id_type=MESH,
            )
            copy.start()
            copies.append(copy)

    root = jnp.sqrt(cell_area)
    settled = settle[...]
    weights = [courant[face] * orient[face].astype(jnp.float32) for face in range(3)]
    keep = root * (1.0 - settled - weights[0] - weights[1] - weights[2])
    fall = root * settled
    grown = root * cell_area
    fluxes = [grown * weight for weight in weights]

    for tile in range(cells // TILE):
        columns = pl.ds(tile * TILE, TILE)
        here = slice(tile * TILE, (tile + 1) * TILE)
        for face in range(3):
            hot = jnp.where(
                lax.broadcasted_iota(jnp.int32, (cells, TILE), 0) == slots[pl.ds(face, 1), columns],
                one, zero,
            )
            other = jnp.dot(v[...], hot, preferred_element_type=jnp.float32)
            for layer in range(layers):
                rows = pl.ds(layer * width, width)
                term = fluxes[face][layer : layer + 1, here] * other[layer * width : (layer + 1) * width]
                if face == 0:
                    lam = probes[rows, columns].astype(jnp.float32)
                    term = term + keep[layer : layer + 1, here] * lam
                    if layer < layers - 1:
                        lower = probes[pl.ds((layer + 1) * width, width), columns]
                        term = term + fall[layer : layer + 1, here] * lower.astype(jnp.float32)
                    total[rows, columns] = term
                else:
                    total[rows, columns] += term

    for chunk in range(chunks):
        for side in range(2):
            rows = pl.ds(chunk * TILE, TILE)
            pltpu.make_async_remote_copy(
                src_ref=outgoing.at[side, rows, :],
                dst_ref=ghosts.at[side, rows, :],
                send_sem=halo_send.at[side, chunk],
                recv_sem=halo_recv.at[side, chunk],
                device_id=(right,),
                device_id_type=MESH,
            ).wait_recv()

    for tile in range(cells // TILE):
        columns = pl.ds(tile * TILE, TILE)
        here = slice(tile * TILE, (tile + 1) * TILE)
        for face in range(3):
            place_of = slots[pl.ds(face, 1), columns] - cells
            other = None
            for side in range(2):
                hot = jnp.where(
                    lax.broadcasted_iota(jnp.int32, (halo, TILE), 0) + side * halo == place_of, one, zero
                )
                product = jnp.dot(ghosts[side], hot, preferred_element_type=jnp.float32)
                other = product if other is None else other + product
            for layer in range(layers):
                rows = pl.ds(layer * width, width)
                term = fluxes[face][layer : layer + 1, here] * other[layer * width : (layer + 1) * width]
                term = total[rows, columns] + term
                if face < 2:
                    total[rows, columns] = term
                else:
                    high = term.astype(jnp.bfloat16)
                    low = (term - high.astype(jnp.float32)).astype(jnp.bfloat16)
                    pairs[layer // 2, pl.ds((layer % 2) * 2 * width, width), columns] = high
                    pairs[layer // 2, pl.ds((layer % 2) * 2 * width + width, width), columns] = low

    stores = []
    for pair in range(layers // 2):
        copy = pltpu.make_async_copy(pairs.at[pair], pairs_out.at[pair], store_sem.at[pair])
        copy.start()
        stores.append(copy)

    square = None
    for pair in range(layers // 2):
        rows = pairs[pair]
        product = lax.dot_general(rows, rows, NT, preferred_element_type=jnp.float32)
        square = product if square is None else square + product
    w = width
    gram = None
    for layer in range(2):
        for a in range(2):
            for b in range(2):
                r, c = (2 * layer + a) * w, (2 * layer + b) * w
                piece = square[r : r + w, c : c + w]
                gram = piece if gram is None else gram + piece
    folded = jnp.concatenate([gram[: w // 2], gram[w // 2 :]], axis=1)
    lines = parts.shape[1]
    for index in range(GROUP):
        parts[index] = folded[index * lines : (index + 1) * lines]

    def exchange(phase, source, target_of, receive, slot):
        def begin(step, _):
            pltpu.make_async_remote_copy(
                src_ref=source(step),
                dst_ref=receive.at[slot],
                send_sem=send_sem.at[phase],
                recv_sem=recv_sem.at[phase],
                device_id=(target_of(step),),
                device_id_type=MESH,
            ).start()
            return 0

        lax.fori_loop(1, GROUP, begin, 0)
        everything = receive.at[pl.ds(0, GROUP - 1)]
        pltpu.make_async_copy(everything, everything, recv_sem.at[phase]).wait()

    def near(step):
        return base + lax.rem(place + step, GROUP)

    def far(step):
        return lax.rem(block + step, others) * GROUP + place

    def add_up(receive):
        terms = [receive[index] for index in range(GROUP)]
        while len(terms) > 1:
            terms = [a + b for a, b in zip(terms[::2], terms[1::2])]
        return terms[0]

    exchange(0, lambda step: parts.at[lax.rem(place + step, GROUP)], near, recv_a, place)
    recv_a[place] = parts[place]
    recv_b[block] = add_up(recv_a)
    exchange(1, lambda step: recv_b.at[block], far, recv_b, block)
    recv_c[place] = add_up(recv_b)
    exchange(2, lambda step: recv_c.at[place], near, recv_c, place)
    gram_out[...] = recv_c[...]

    for phase, buffer in ((0, recv_a), (1, recv_b), (2, recv_c)):
        everything = buffer.at[pl.ds(0, GROUP - 1)]
        pltpu.make_async_copy(everything, everything, send_sem.at[phase]).wait()
    for copy in copies:
        copy.wait_send()
    for copy in stores:
        copy.wait()


def basis_kernel(scale, pairs, gram, basis, factor, loaded, finished, load_sem, store_sem):
    groups = pairs.shape[0]
    width = factor.shape[0]
    loads = []
    for group in range(groups):
        copy = pltpu.make_async_copy(pairs.at[group], loaded.at[group], load_sem.at[group])
        copy.start()
        loads.append(copy)

    folded = jnp.concatenate([gram[index] for index in range(gram.shape[0])], axis=0)
    whole = jnp.concatenate([folded[:, :width], folded[:, width:]], axis=0)
    row = lax.broadcasted_iota(jnp.int32, (width, 2 * width), 0)
    lane = lax.broadcasted_iota(jnp.int32, (width, 2 * width), 1)
    unit = (lax.broadcasted_iota(jnp.int32, (width, width), 0)
            == lax.broadcasted_iota(jnp.int32, (width, width), 1)).astype(jnp.float32)
    work = jnp.concatenate([whole, unit], axis=1)
    strips = [work[8 * i : 8 * i + 8] for i in range(width // 8)]
    low_row = lax.broadcasted_iota(jnp.int32, (8, 1), 0)
    for step in range(width):
        home, inner = step // 8, step % 8
        line = strips[home][inner : inner + 1]
        line = line * (1.0 / line[:, step : step + 1])
        for strip in range(home, width // 8):
            column = strips[strip][:, step : step + 1]
            if strip == home:
                column = jnp.where(low_row > inner, column, 0.0)
            strips[strip] = strips[strip] - column * line
    work = jnp.concatenate(strips, axis=0)
    pivots = jnp.sum(jnp.where(lane == row, work, 0.0), axis=1, keepdims=True)
    work = work / jnp.sqrt(pivots)
    factor[...] = jnp.where(lane >= row, work, 0.0)[:, :width] / scale
    inverse = jnp.where(lane - width <= row, work, 0.0)[:, width:] * scale
    high = inverse.astype(jnp.bfloat16)
    low = (inverse - high.astype(jnp.float32)).astype(jnp.bfloat16)
    none = jnp.zeros_like(high)

    def spread(block):
        return jnp.concatenate([
            jnp.concatenate([block, block, none, none], axis=1),
            jnp.concatenate([none, none, block, block], axis=1),
        ], axis=0)

    lead, rest = spread(high), spread(low)
    stores = []
    for group in range(groups):
        loads[group].wait()
        rows = loaded[group]
        result = jnp.dot(lead, rows, preferred_element_type=jnp.float32)
        result += jnp.dot(rest, rows, preferred_element_type=jnp.float32)
        finished[group] = result
        copy = pltpu.make_async_copy(finished.at[group], basis.at[group], store_sem.at[group])
        copy.start()
        stores.append(copy)
    for copy in stores:
        copy.wait()


def body(probes, area, settle, courant, orient, local_slot, send_rows):
    layers, width, cells = probes.shape
    halo = send_rows.shape[0] // 2
    devices = lax.axis_size("cells")
    groups = layers // 2
    lines = width * width // (GROUP * 2 * width)
    vmem = pl.BlockSpec(memory_space=pltpu.VMEM)
    anywhere = pl.BlockSpec(memory_space=pl.ANY)
    chunks = layers * width // TILE
    flat = probes.reshape(layers * width, cells)
    pairs, gram = pl.pallas_call(
        functools.partial(advect_kernel, devices),
        out_shape=(
            jax.ShapeDtypeStruct((groups, 4 * width, cells), jnp.bfloat16),
            jax.ShapeDtypeStruct((GROUP, lines, 2 * width), jnp.float32),
        ),
        in_specs=[vmem] * 7,
        out_specs=(anywhere, vmem),
        scratch_shapes=[
            pltpu.VMEM((layers * width, cells), jnp.bfloat16),
            pltpu.VMEM((2, layers * width, halo), jnp.bfloat16),
            pltpu.VMEM((2, layers * width, halo), jnp.bfloat16),
            pltpu.VMEM((layers * width, cells), jnp.float32),
            pltpu.VMEM((groups, 4 * width, cells), jnp.bfloat16),
            pltpu.VMEM((GROUP, lines, 2 * width), jnp.float32),
            pltpu.VMEM((GROUP, lines, 2 * width), jnp.float32),
            pltpu.VMEM((GROUP, lines, 2 * width), jnp.float32),
            pltpu.VMEM((GROUP, lines, 2 * width), jnp.float32),
            pltpu.SemaphoreType.DMA((2, chunks)),
            pltpu.SemaphoreType.DMA((2, chunks)),
            pltpu.SemaphoreType.DMA((3,)),
            pltpu.SemaphoreType.DMA((3,)),
            pltpu.SemaphoreType.DMA((groups,)),
        ],
        compiler_params=pltpu.CompilerParams(
            collective_id=0, has_side_effects=True, vmem_limit_bytes=44 * 2**20
        ),
        name="advect",
    )(flat, area[None, :], settle, courant, orient, local_slot, send_rows[None, :])
    scale = math.sqrt(layers * cells * devices)
    basis, factor = pl.pallas_call(
        functools.partial(basis_kernel, scale),
        out_shape=(
            jax.ShapeDtypeStruct((groups, 2 * width, cells), jnp.float32),
            jax.ShapeDtypeStruct((width, width), jnp.float32),
        ),
        in_specs=[anywhere, vmem],
        out_specs=(anywhere, vmem),
        scratch_shapes=[
            pltpu.VMEM((groups, 4 * width, cells), jnp.bfloat16),
            pltpu.VMEM((groups, 2 * width, cells), jnp.float32),
            pltpu.SemaphoreType.DMA((groups,)),
            pltpu.SemaphoreType.DMA((groups,)),
        ],
        compiler_params=pltpu.CompilerParams(vmem_limit_bytes=24 * 2**20),
        name="basis",
    )(pairs, gram)
    return basis.reshape(layers, width, cells), factor


def solution(mesh):
    in_specs = (
        P(None, None, "cells"),
        P("cells"),
        P(None, "cells"),
        P(None, None, "cells"),
        P(None, None, "cells"),
        P(None, "cells"),
        P("cells"),
    )
    out_specs = (P(None, None, "cells"), P())
    return jax.shard_map(body, mesh=mesh, in_specs=in_specs, out_specs=out_specs, check_vma=False)
```

```python
import functools
import itertools
import math

import jax
import jax.numpy as jnp
from jax import lax
from jax.experimental import pallas as pl
from jax.experimental.pallas import tpu as pltpu
from jax.sharding import PartitionSpec as P

MESH = pl.DeviceIdType.MESH
Y, X, Z = 4, 4, 8
CHUNK = 512
NT = (((1,), (1,)), ((), ()))


def far_first(*sizes):
    offsets = itertools.product(*(range(size) for size in sizes))
    away = lambda offset: sum(min(o, s - o) for o, s in zip(offset, sizes))
    ordered = sorted((o for o in offsets if any(o)), key=away, reverse=True)
    return ordered if len(sizes) > 1 else [o for o, in ordered]


def advect_kernel(
    devices, probes_in, area_in, settle_in, courant_in, orient_in, slots_in, sends_in,
    pairs, gram_out,
    probes, area, settle, courant, orient, slots, sends,
    v, outgoing, ghosts, total, halves, from_core, along_z, along_xy, final,
    load_sem, halo_send, halo_recv, send_sem, recv_sem,
):
    layers, cells = settle.shape
    width = probes.shape[0] // layers
    halo = sends.shape[1] // 2
    chunks = probes.shape[0] // CHUNK
    me = lax.axis_index("cells")
    left, right = lax.rem(me + devices - 1, devices), lax.rem(me + 1, devices)
    core, z, block = lax.rem(me, 2), lax.rem(me // 2, Z), me // (2 * Z)
    y, x = block // X, lax.rem(block, X)
    sibling = me + 1 - 2 * core
    z_peers = [me + 2 * (lax.rem(z + step, Z) - z) for step in far_first(Z)]
    xy_peers = [
        (lax.rem(y + dy, Y) * X + lax.rem(x + dx, X)) * 2 * Z + z * 2 + core
        for dy, dx in far_first(Y, X)
    ]

    loads = {}
    for index, (name, source, target) in enumerate((
        ("sends", sends_in, sends), ("area", area_in, area), ("probes", probes_in, probes),
        ("slots", slots_in, slots), ("courant", courant_in, courant),
        ("orient", orient_in, orient), ("settle", settle_in, settle),
    )):
        loads[name] = pltpu.make_async_copy(source, target, load_sem.at[index])
        loads[name].start()

    barrier = pltpu.get_barrier_semaphore()
    greeted = [left, right, sibling] + z_peers + xy_peers
    for peer in greeted:
        pl.semaphore_signal(barrier, inc=1, device_id=(peer,), device_id_type=MESH)

    one, zero = jnp.bfloat16(1), jnp.bfloat16(0)
    loads["sends"].wait()
    pick = jnp.where(
        lax.broadcasted_iota(jnp.int32, (cells, 2 * halo), 0) == sends[...], one, zero
    )
    loads["area"].wait()
    cell_area = area[...]
    inverse_area = 1.0 / cell_area
    loads["probes"].wait()
    copies, arrivals = [], []
    for chunk in range(chunks):
        rows = pl.ds(chunk * CHUNK, CHUNK)
        part = (probes[rows, :].astype(jnp.float32) * inverse_area).astype(jnp.bfloat16)
        v[rows, :] = part
        picked = jnp.dot(part, pick, preferred_element_type=jnp.float32).astype(jnp.bfloat16)
        outgoing[0, rows, :] = picked[:, :halo]
        outgoing[1, rows, :] = picked[:, halo:]
        if chunk == 0:
            pl.semaphore_wait(barrier, len(greeted))
        for side, target in ((0, left), (1, right)):
            copy = pltpu.make_async_remote_copy(
                src_ref=outgoing.at[side, rows, :],
                dst_ref=ghosts.at[rows, pl.ds((1 - side) * halo, halo)],
                send_sem=halo_send.at[side, chunk],
                recv_sem=halo_recv.at[1 - side, chunk],
                device_id=(target,),
                device_id_type=MESH,
            )
            copy.start()
            copies.append(copy)
            arrivals.append(pltpu.make_async_copy(
                outgoing.at[side, rows, :], ghosts.at[rows, pl.ds(side * halo, halo)], halo_recv.at[side, chunk]
            ))

    for name in ("slots", "courant", "orient", "settle"):
        loads[name].wait()
    root = jnp.sqrt(cell_area)
    settled = settle[...]
    weights = [courant[face] * orient[face].astype(jnp.float32) for face in range(3)]
    keep = root * (1.0 - settled - weights[0] - weights[1] - weights[2])
    fall = root * settled
    grown = root * cell_area
    fluxes = [grown * weight for weight in weights]

    for face in range(3):
        hot = jnp.where(
            lax.broadcasted_iota(jnp.int32, (cells, cells), 0) == slots[pl.ds(face, 1), :], one, zero
        )
        other = jnp.dot(v[...], hot, preferred_element_type=jnp.float32)
        for layer in range(layers):
            rows = pl.ds(layer * width, width)
            term = fluxes[face][layer : layer + 1] * other[layer * width : (layer + 1) * width]
            if face == 0:
                term = term + keep[layer : layer + 1] * probes[rows, :].astype(jnp.float32)
                if layer < layers - 1:
                    lower = probes[pl.ds((layer + 1) * width, width), :]
                    term = term + fall[layer : layer + 1] * lower.astype(jnp.float32)
                total[rows, :] = term
            else:
                total[rows, :] += term

    for arrival in arrivals:
        arrival.wait()

    for face in range(3):
        place = slots[pl.ds(face, 1), :] - cells
        hot = jnp.where(
            lax.broadcasted_iota(jnp.int32, (2 * halo, cells), 0) == place, one, zero
        )
        other = jnp.dot(ghosts[...], hot, preferred_element_type=jnp.float32)
        for layer in range(layers):
            rows = pl.ds(layer * width, width)
            term = fluxes[face][layer : layer + 1] * other[layer * width : (layer + 1) * width]
            term = total[rows, :] + term
            if face < 2:
                total[rows, :] = term
            else:
                high = term.astype(jnp.bfloat16)
                low = (term - high.astype(jnp.float32)).astype(jnp.bfloat16)
                pairs[layer // 2, pl.ds((layer % 2) * 2 * width, width), :] = high
                pairs[layer // 2, pl.ds((layer % 2) * 2 * width + width, width), :] = low

    square = None
    for pair in range(layers // 2):
        rows = pairs[pair]
        product = lax.dot_general(rows, rows, NT, preferred_element_type=jnp.float32)
        square = product if square is None else square + product
    w = width
    gram = None
    for layer in range(2):
        for a in range(2):
            for b in range(2):
                r, c = (2 * layer + a) * w, (2 * layer + b) * w
                piece = square[r : r + w, c : c + w]
                gram = piece if gram is None else gram + piece
    folded = jnp.concatenate([gram[: w // 2], gram[w // 2 :]], axis=1)
    halves[0] = folded[: w // 4]
    halves[1] = folded[w // 4 :]

    def send(phase, source, target, peers):
        for peer in peers:
            pltpu.make_async_remote_copy(
                src_ref=source,
                dst_ref=target,
                send_sem=send_sem.at[phase],
                recv_sem=recv_sem.at[phase],
                device_id=(peer,),
                device_id_type=MESH,
            ).start()

    def settle_all(buffer, count, semaphore):
        span = buffer.at[pl.ds(0, count)] if count else buffer
        pltpu.make_async_copy(span, span, semaphore).wait()

    def add_up(receive):
        terms = [receive[index] for index in range(receive.shape[0])]
        while len(terms) > 1:
            terms = [a + b for a, b in zip(terms[::2], terms[1::2])]
        return terms[0]

    send(0, halves.at[1 - core], from_core, [sibling])
    settle_all(from_core, 0, recv_sem.at[0])
    along_z[z] = halves[core] + from_core[...]
    send(1, along_z.at[z], along_z.at[z], z_peers)
    settle_all(along_z, Z - 1, recv_sem.at[1])
    along_xy[block] = add_up(along_z)
    send(2, along_xy.at[block], along_xy.at[block], xy_peers)
    settle_all(along_xy, X * Y - 1, recv_sem.at[2])
    final[core] = add_up(along_xy)
    send(3, final.at[core], final.at[core], [sibling])
    settle_all(from_core, 0, recv_sem.at[3])
    gram_out[...] = final[...]

    settle_all(from_core, 0, send_sem.at[0])
    settle_all(along_z, Z - 1, send_sem.at[1])
    settle_all(along_xy, X * Y - 1, send_sem.at[2])
    settle_all(from_core, 0, send_sem.at[3])
    for copy in copies:
        copy.wait_send()


def factorize(strips, width):
    full = (8, 2 * width)
    row = lax.broadcasted_iota(jnp.int32, full, 0)
    strips, finished = list(strips), []

    def lane(values, index):
        return jnp.take_along_axis(values, jnp.full(full, index, jnp.int32), axis=1)

    def line(values, index):
        return jnp.broadcast_to(values[index : index + 1], full)

    for home in range(width // 8):
        step = 8 * home
        mine = strips[home]
        upper = [line(mine, p) for p in range(8)]
        block = [[None] * 8 for _ in range(8)]
        for q in range(8):
            column = lane(mine, step + q)
            for p in range(q + 1):
                block[p][q] = line(column, p)
        ratio = [[None] * 8 for _ in range(8)]
        scaled = []
        for p in range(8):
            reciprocal = 1.0 / block[p][p]
            for q in range(p + 1, 8):
                ratio[q][p] = block[p][q] * reciprocal
            for q in range(p + 1, 8):
                for t in range(q, 8):
                    block[q][t] = block[q][t] - ratio[q][p] * block[p][t]
                upper[q] = upper[q] - ratio[q][p] * upper[p]
            scaled.append(upper[p] * reciprocal)
        for strip in range(home + 1, width // 8):
            columns = [lane(strips[strip], step + q) for q in range(8)]
            for p in range(8):
                for q in range(p + 1, 8):
                    columns[q] = columns[q] - ratio[q][p] * columns[p]
            terms = [c * n for c, n in zip(columns, scaled)]
            while len(terms) > 1:
                terms = [a + b for a, b in zip(terms[::2], terms[1::2])]
            strips[strip] = strips[strip] - terms[0]
        done = None
        for p in range(8):
            scaled_row = upper[p] / jnp.sqrt(block[p][p])
            done = scaled_row if done is None else jnp.where(row == p, scaled_row, done)
        finished.append(done)
    return finished


def basis_kernel(scale, pairs, gram, basis, factor, results, store_sem):
    groups = pairs.shape[0]
    width = factor.shape[0]
    folded = jnp.concatenate([gram[0], gram[1]], axis=0)
    whole = jnp.concatenate([folded[:, :width], folded[:, width:]], axis=0)
    unit = (lax.broadcasted_iota(jnp.int32, (width, width), 0)
            == lax.broadcasted_iota(jnp.int32, (width, width), 1)).astype(jnp.float32)
    work = jnp.concatenate([whole, unit], axis=1)
    work = jnp.concatenate(factorize([work[8 * i : 8 * i + 8] for i in range(width // 8)], width), axis=0)
    row = lax.broadcasted_iota(jnp.int32, (width, 2 * width), 0)
    lane = lax.broadcasted_iota(jnp.int32, (width, 2 * width), 1)
    factor[...] = jnp.where(lane >= row, work, 0.0)[:, :width] / scale
    inverse = jnp.where(lane - width <= row, work, 0.0)[:, width:] * scale
    high = inverse.astype(jnp.bfloat16)
    low = (inverse - high.astype(jnp.float32)).astype(jnp.bfloat16)
    none = jnp.zeros_like(high)

    def spread(block):
        return [
            jnp.concatenate([block, block, none, none], axis=1),
            jnp.concatenate([none, none, block, block], axis=1),
        ]

    stacked = jnp.concatenate(spread(high) + spread(low), axis=0)
    stores = []
    for group in range(groups):
        product = jnp.dot(stacked, pairs[group], preferred_element_type=jnp.float32)
        results[group] = product[: 2 * width] + product[2 * width :]
        copy = pltpu.make_async_copy(results.at[group], basis.at[group], store_sem.at[group])
        copy.start()
        stores.append(copy)
    for copy in stores:
        copy.wait()


def body(probes, area, settle, courant, orient, local_slot, send_rows):
    layers, width, cells = probes.shape
    halo = send_rows.shape[0] // 2
    devices = lax.axis_size("cells")
    groups = layers // 2
    vmem = pl.BlockSpec(memory_space=pltpu.VMEM)
    hbm = pl.BlockSpec(memory_space=pltpu.HBM)
    chunks = layers * width // CHUNK
    inputs = (
        probes.reshape(layers * width, cells), area[None, :], settle, courant, orient,
        local_slot, send_rows[None, :],
    )
    half = (width // 4, 2 * width)
    pairs, gram = pl.pallas_call(
        functools.partial(advect_kernel, devices),
        out_shape=(
            jax.ShapeDtypeStruct((groups, 4 * width, cells), jnp.bfloat16),
            jax.ShapeDtypeStruct((2, *half), jnp.float32),
        ),
        in_specs=[hbm] * 7,
        out_specs=(vmem, vmem),
        scratch_shapes=[pltpu.VMEM(array.shape, array.dtype) for array in inputs] + [
            pltpu.VMEM((layers * width, cells), jnp.bfloat16),
            pltpu.VMEM((2, layers * width, halo), jnp.bfloat16),
            pltpu.VMEM((layers * width, 2 * halo), jnp.bfloat16),
            pltpu.VMEM((layers * width, cells), jnp.float32),
            pltpu.VMEM((2, *half), jnp.float32),
            pltpu.VMEM(half, jnp.float32),
            pltpu.VMEM((Z, *half), jnp.float32),
            pltpu.VMEM((X * Y, *half), jnp.float32),
            pltpu.VMEM((2, *half), jnp.float32),
            pltpu.SemaphoreType.DMA((7,)),
            pltpu.SemaphoreType.DMA((2, chunks)),
            pltpu.SemaphoreType.DMA((2, chunks)),
            pltpu.SemaphoreType.DMA((4,)),
            pltpu.SemaphoreType.DMA((4,)),
        ],
        compiler_params=pltpu.CompilerParams(
            collective_id=0, has_side_effects=True, vmem_limit_bytes=44 * 2**20
        ),
        name="advect",
    )(*(pltpu.with_memory_space_constraint(array, pltpu.HBM) for array in inputs))
    scale = math.sqrt(layers * cells * devices)
    basis, factor = pl.pallas_call(
        functools.partial(basis_kernel, scale),
        out_shape=(
            jax.ShapeDtypeStruct((groups, 2 * width, cells), jnp.float32),
            jax.ShapeDtypeStruct((width, width), jnp.float32),
        ),
        in_specs=[vmem, vmem],
        out_specs=(hbm, vmem),
        scratch_shapes=[
            pltpu.VMEM((groups, 2 * width, cells), jnp.float32),
            pltpu.SemaphoreType.DMA((groups,)),
        ],
        compiler_params=pltpu.CompilerParams(vmem_limit_bytes=24 * 2**20),
        name="basis",
    )(pairs, gram)
    return basis.reshape(layers, width, cells), factor


def solution(mesh):
    in_specs = (
        P(None, None, "cells"),
        P("cells"),
        P(None, "cells"),
        P(None, None, "cells"),
        P(None, None, "cells"),
        P(None, "cells"),
        P("cells"),
    )
    out_specs = (P(None, None, "cells"), P())
    return jax.shard_map(body, mesh=mesh, in_specs=in_specs, out_specs=out_specs, check_vma=False)
```

```python
import functools
import itertools
import math

import jax
import jax.numpy as jnp
from jax import lax
from jax.experimental import pallas as pl
from jax.experimental.pallas import tpu as pltpu
from jax.sharding import PartitionSpec as P

MESH = pl.DeviceIdType.MESH
Y, X, Z = 4, 4, 8
SENT = (128, 128, 256, 256, 256)
CHUNK = 256
NT = (((1,), (1,)), ((), ()))


def far_first(*sizes):
    offsets = itertools.product(*(range(size) for size in sizes))
    away = lambda offset: sum(min(o, s - o) for o, s in zip(offset, sizes))
    ordered = sorted((o for o in offsets if any(o)), key=away, reverse=True)
    return ordered if len(sizes) > 1 else [o for o, in ordered]


def advect_kernel(
    devices, probes_in, area_in, settle_in, courant_in, orient_in, slots_in, sends_in,
    pairs, gram_out,
    probes, area, settle, courant, orient, slots, sends,
    v, outgoing, ghosts, hots, total, halves, from_core, along_z, along_xy, final,
    load_sem, halo_send, halo_recv, send_sem, recv_sem,
):
    layers, cells = settle.shape
    width = probes.shape[0] // layers
    halo = sends.shape[1] // 2
    me = lax.axis_index("cells")
    left, right = lax.rem(me + devices - 1, devices), lax.rem(me + 1, devices)
    core, z, block = lax.rem(me, 2), lax.rem(me // 2, Z), me // (2 * Z)
    y, x = block // X, lax.rem(block, X)
    sibling = me + 1 - 2 * core
    z_peers = [me + 2 * (lax.rem(z + step, Z) - z) for step in far_first(Z)]
    xy_peers = [
        (lax.rem(y + dy, Y) * X + lax.rem(x + dx, X)) * 2 * Z + z * 2 + core
        for dy, dx in far_first(Y, X)
    ]

    loads = {}
    starts = [sum(SENT[:chunk]) for chunk in range(len(SENT))]
    spans = [pl.ds(start, size) for start, size in zip(starts, SENT)]
    plan = [("sends", sends_in, sends), ("area", area_in, area)]
    plan += [(chunk, probes_in.at[span], probes.at[span]) for chunk, span in enumerate(spans)]
    plan += [
        ("slots", slots_in, slots), ("courant", courant_in, courant),
        ("orient", orient_in, orient), ("settle", settle_in, settle),
    ]
    for index, (name, source, target) in enumerate(plan):
        loads[name] = pltpu.make_async_copy(source, target, load_sem.at[index])
        loads[name].start()

    barrier = pltpu.get_barrier_semaphore()
    greeted = [left, right, sibling] + z_peers + xy_peers
    for peer in greeted:
        pl.semaphore_signal(barrier, inc=1, device_id=(peer,), device_id_type=MESH)

    one, zero = jnp.bfloat16(1), jnp.bfloat16(0)
    loads["sends"].wait()
    pick = jnp.where(
        lax.broadcasted_iota(jnp.int32, (cells, 2 * halo), 0) == sends[...], one, zero
    )
    loads["area"].wait()
    cell_area = area[...]
    inverse_area = 1.0 / cell_area
    copies, arrivals = [], []
    for chunk, rows in enumerate(spans):
        loads[chunk].wait()
        part = (probes[rows, :].astype(jnp.float32) * inverse_area).astype(jnp.bfloat16)
        v[rows, :] = part
        picked = jnp.dot(part, pick, preferred_element_type=jnp.float32).astype(jnp.bfloat16)
        outgoing[0, rows, :] = picked[:, :halo]
        outgoing[1, rows, :] = picked[:, halo:]
        if chunk == 0:
            pl.semaphore_wait(barrier, len(greeted))
        for side, target in ((0, left), (1, right)):
            copy = pltpu.make_async_remote_copy(
                src_ref=outgoing.at[side, rows, :],
                dst_ref=ghosts.at[rows, pl.ds((1 - side) * halo, halo)],
                send_sem=halo_send.at[side, chunk],
                recv_sem=halo_recv.at[1 - side, chunk],
                device_id=(target,),
                device_id_type=MESH,
            )
            copy.start()
            copies.append(copy)
            arrivals.append(pltpu.make_async_copy(
                outgoing.at[side, rows, :], ghosts.at[rows, pl.ds(side * halo, halo)], halo_recv.at[side, chunk]
            ))

    for name in ("slots", "courant", "orient", "settle"):
        loads[name].wait()
    root = jnp.sqrt(cell_area)
    settled = settle[...]
    weights = [courant[face] * orient[face].astype(jnp.float32) for face in range(3)]
    keep = root * (1.0 - settled - weights[0] - weights[1] - weights[2])
    fall = root * settled
    grown = root * cell_area
    fluxes = [grown * weight for weight in weights]

    for face in range(3):
        hot = jnp.where(
            lax.broadcasted_iota(jnp.int32, (cells, cells), 0) == slots[pl.ds(face, 1), :], one, zero
        )
        place = slots[pl.ds(face, 1), :] - cells
        hots[face] = jnp.where(
            lax.broadcasted_iota(jnp.int32, (2 * halo, cells), 0) == place, one, zero
        )
        other = jnp.dot(v[...], hot, preferred_element_type=jnp.float32)
        for layer in range(layers):
            rows = pl.ds(layer * width, width)
            term = fluxes[face][layer : layer + 1] * other[layer * width : (layer + 1) * width]
            if face == 0:
                term = term + keep[layer : layer + 1] * probes[rows, :].astype(jnp.float32)
                if layer < layers - 1:
                    lower = probes[pl.ds((layer + 1) * width, width), :]
                    term = term + fall[layer : layer + 1] * lower.astype(jnp.float32)
                total[rows, :] = term
            else:
                total[rows, :] += term

    def square_of(chunk):
        first = chunk * CHUNK // (2 * width)
        product = None
        for pair in range(first, first + CHUNK // (2 * width)):
            rows = pairs[pair]
            term = lax.dot_general(rows, rows, NT, preferred_element_type=jnp.float32)
            product = term if product is None else product + term
        return product

    for arrival in arrivals:
        arrival.wait()
    square = None
    for chunk in range(probes.shape[0] // CHUNK):
        rows = ghosts[pl.ds(chunk * CHUNK, CHUNK), :]
        others = [jnp.dot(rows, hots[face], preferred_element_type=jnp.float32) for face in range(3)]
        if chunk:
            product = square_of(chunk - 1)
            square = product if square is None else square + product
        for inner in range(CHUNK // width):
            layer = chunk * (CHUNK // width) + inner
            term = total[pl.ds(layer * width, width), :]
            for face in range(3):
                other = others[face][inner * width : (inner + 1) * width]
                term = term + fluxes[face][layer : layer + 1] * other
            high = term.astype(jnp.bfloat16)
            low = (term - high.astype(jnp.float32)).astype(jnp.bfloat16)
            pairs[layer // 2, pl.ds((layer % 2) * 2 * width, width), :] = high
            pairs[layer // 2, pl.ds((layer % 2) * 2 * width + width, width), :] = low
    square = square + square_of(probes.shape[0] // CHUNK - 1)
    w = width
    gram = None
    for layer in range(2):
        for a in range(2):
            for b in range(2):
                r, c = (2 * layer + a) * w, (2 * layer + b) * w
                piece = square[r : r + w, c : c + w]
                gram = piece if gram is None else gram + piece
    folded = jnp.concatenate([gram[: w // 2], gram[w // 2 :]], axis=1)
    halves[0] = folded[: w // 4]
    halves[1] = folded[w // 4 :]

    def send(phase, source, target, peers):
        for peer in peers:
            pltpu.make_async_remote_copy(
                src_ref=source,
                dst_ref=target,
                send_sem=send_sem.at[phase],
                recv_sem=recv_sem.at[phase],
                device_id=(peer,),
                device_id_type=MESH,
            ).start()

    def settle_all(buffer, count, semaphore):
        span = buffer.at[pl.ds(0, count)] if count else buffer
        pltpu.make_async_copy(span, span, semaphore).wait()

    def add_up(receive):
        terms = [receive[index] for index in range(receive.shape[0])]
        while len(terms) > 1:
            terms = [a + b for a, b in zip(terms[::2], terms[1::2])]
        return terms[0]

    send(0, halves.at[1 - core], from_core, [sibling])
    settle_all(from_core, 0, recv_sem.at[0])
    along_z[z] = halves[core] + from_core[...]
    send(1, along_z.at[z], along_z.at[z], z_peers)
    settle_all(along_z, Z - 1, recv_sem.at[1])
    along_xy[block] = add_up(along_z)
    send(2, along_xy.at[block], along_xy.at[block], xy_peers)
    settle_all(along_xy, X * Y - 1, recv_sem.at[2])
    final[core] = add_up(along_xy)
    send(3, final.at[core], final.at[core], [sibling])
    settle_all(from_core, 0, recv_sem.at[3])
    gram_out[...] = final[...]

    settle_all(from_core, 0, send_sem.at[0])
    settle_all(along_z, Z - 1, send_sem.at[1])
    settle_all(along_xy, X * Y - 1, send_sem.at[2])
    settle_all(from_core, 0, send_sem.at[3])
    for copy in copies:
        copy.wait_send()


def factorize(strips, width):
    full = (8, 2 * width)
    row = lax.broadcasted_iota(jnp.int32, full, 0)
    strips, finished = list(strips), []

    def lane(values, index):
        return jnp.take_along_axis(values, jnp.full(full, index, jnp.int32), axis=1)

    def line(values, index):
        return jnp.broadcast_to(values[index : index + 1], full)

    for home in range(width // 8):
        step = 8 * home
        mine = strips[home]
        upper = [line(mine, p) for p in range(8)]
        block = [[None] * 8 for _ in range(8)]
        for q in range(8):
            column = lane(mine, step + q)
            for p in range(q + 1):
                block[p][q] = line(column, p)
        ratio = [[None] * 8 for _ in range(8)]
        scaled = []
        for p in range(8):
            reciprocal = 1.0 / block[p][p]
            for q in range(p + 1, 8):
                ratio[q][p] = block[p][q] * reciprocal
            for q in range(p + 1, 8):
                for t in range(q, 8):
                    block[q][t] = block[q][t] - ratio[q][p] * block[p][t]
                upper[q] = upper[q] - ratio[q][p] * upper[p]
            scaled.append(upper[p] * reciprocal)
        for strip in range(home + 1, width // 8):
            columns = [lane(strips[strip], step + q) for q in range(8)]
            for p in range(8):
                for q in range(p + 1, 8):
                    columns[q] = columns[q] - ratio[q][p] * columns[p]
            terms = [c * n for c, n in zip(columns, scaled)]
            while len(terms) > 1:
                terms = [a + b for a, b in zip(terms[::2], terms[1::2])]
            strips[strip] = strips[strip] - terms[0]
        done = None
        for p in range(8):
            scaled_row = upper[p] / jnp.sqrt(block[p][p])
            done = scaled_row if done is None else jnp.where(row == p, scaled_row, done)
        finished.append(done)
    return finished


def basis_kernel(scale, pairs, gram, basis, factor, results, store_sem):
    groups = pairs.shape[0]
    width = factor.shape[0]
    folded = jnp.concatenate([gram[0], gram[1]], axis=0)
    whole = jnp.concatenate([folded[:, :width], folded[:, width:]], axis=0)
    unit = (lax.broadcasted_iota(jnp.int32, (width, width), 0)
            == lax.broadcasted_iota(jnp.int32, (width, width), 1)).astype(jnp.float32)
    work = jnp.concatenate([whole, unit], axis=1)
    work = jnp.concatenate(factorize([work[8 * i : 8 * i + 8] for i in range(width // 8)], width), axis=0)
    row = lax.broadcasted_iota(jnp.int32, (width, 2 * width), 0)
    lane = lax.broadcasted_iota(jnp.int32, (width, 2 * width), 1)
    factor[...] = jnp.where(lane >= row, work, 0.0)[:, :width] / scale
    inverse = jnp.where(lane - width <= row, work, 0.0)[:, width:] * scale
    high = inverse.astype(jnp.bfloat16)
    low = (inverse - high.astype(jnp.float32)).astype(jnp.bfloat16)
    none = jnp.zeros_like(high)

    def spread(block):
        return [
            jnp.concatenate([block, block, none, none], axis=1),
            jnp.concatenate([none, none, block, block], axis=1),
        ]

    stacked = jnp.concatenate(spread(high) + spread(low), axis=0)
    stores = []
    for group in range(groups):
        product = jnp.dot(stacked, pairs[group], preferred_element_type=jnp.float32)
        results[group] = product[: 2 * width] + product[2 * width :]
        copy = pltpu.make_async_copy(results.at[group], basis.at[group], store_sem.at[group])
        copy.start()
        stores.append(copy)
    for copy in stores:
        copy.wait()


def body(probes, area, settle, courant, orient, local_slot, send_rows):
    layers, width, cells = probes.shape
    halo = send_rows.shape[0] // 2
    devices = lax.axis_size("cells")
    groups = layers // 2
    vmem = pl.BlockSpec(memory_space=pltpu.VMEM)
    hbm = pl.BlockSpec(memory_space=pltpu.HBM)
    sent = len(SENT)
    inputs = (
        probes.reshape(layers * width, cells), area[None, :], settle, courant, orient,
        local_slot, send_rows[None, :],
    )
    half = (width // 4, 2 * width)
    pairs, gram = pl.pallas_call(
        functools.partial(advect_kernel, devices),
        out_shape=(
            jax.ShapeDtypeStruct((groups, 4 * width, cells), jnp.bfloat16),
            jax.ShapeDtypeStruct((2, *half), jnp.float32),
        ),
        in_specs=[hbm] * 7,
        out_specs=(vmem, vmem),
        scratch_shapes=[pltpu.VMEM(array.shape, array.dtype) for array in inputs] + [
            pltpu.VMEM((layers * width, cells), jnp.bfloat16),
            pltpu.VMEM((2, layers * width, halo), jnp.bfloat16),
            pltpu.VMEM((layers * width, 2 * halo), jnp.bfloat16),
            pltpu.VMEM((3, 2 * halo, cells), jnp.bfloat16),
            pltpu.VMEM((layers * width, cells), jnp.float32),
            pltpu.VMEM((2, *half), jnp.float32),
            pltpu.VMEM(half, jnp.float32),
            pltpu.VMEM((Z, *half), jnp.float32),
            pltpu.VMEM((X * Y, *half), jnp.float32),
            pltpu.VMEM((2, *half), jnp.float32),
            pltpu.SemaphoreType.DMA((6 + sent,)),
            pltpu.SemaphoreType.DMA((2, sent)),
            pltpu.SemaphoreType.DMA((2, sent)),
            pltpu.SemaphoreType.DMA((4,)),
            pltpu.SemaphoreType.DMA((4,)),
        ],
        compiler_params=pltpu.CompilerParams(
            collective_id=0, has_side_effects=True, vmem_limit_bytes=44 * 2**20
        ),
        name="advect",
    )(*(pltpu.with_memory_space_constraint(array, pltpu.HBM) for array in inputs))
    scale = math.sqrt(layers * cells * devices)
    basis, factor = pl.pallas_call(
        functools.partial(basis_kernel, scale),
        out_shape=(
            jax.ShapeDtypeStruct((groups, 2 * width, cells), jnp.float32),
            jax.ShapeDtypeStruct((width, width), jnp.float32),
        ),
        in_specs=[vmem, vmem],
        out_specs=(hbm, vmem),
        scratch_shapes=[
            pltpu.VMEM((groups, 2 * width, cells), jnp.float32),
            pltpu.SemaphoreType.DMA((groups,)),
        ],
        compiler_params=pltpu.CompilerParams(vmem_limit_bytes=24 * 2**20),
        name="basis",
    )(pairs, gram)
    return basis.reshape(layers, width, cells), factor


def solution(mesh):
    in_specs = (
        P(None, None, "cells"),
        P("cells"),
        P(None, "cells"),
        P(None, None, "cells"),
        P(None, None, "cells"),
        P(None, "cells"),
        P("cells"),
    )
    out_specs = (P(None, None, "cells"), P())
    return jax.shard_map(body, mesh=mesh, in_specs=in_specs, out_specs=out_specs, check_vma=False)
```

```python
import functools
import itertools
import math

import jax
import jax.numpy as jnp
from jax import lax
from jax.experimental import pallas as pl
from jax.experimental.pallas import tpu as pltpu
from jax.sharding import PartitionSpec as P

MESH = pl.DeviceIdType.MESH
Y, X, Z = 4, 4, 8
SENT = (256, 768)
CHUNK = 256
PARTS = 2
NT = (((1,), (1,)), ((), ()))


def far_first(*sizes):
    offsets = itertools.product(*(range(size) for size in sizes))
    away = lambda offset: sum(min(o, s - o) for o, s in zip(offset, sizes))
    ordered = sorted((o for o in offsets if any(o)), key=away, reverse=True)
    return ordered if len(sizes) > 1 else [o for o, in ordered]


def advect_kernel(
    devices, probes_in, area_in, settle_in, courant_in, orient_in, slots_in, sends_in,
    pairs, gram_out,
    probes, area, settle, courant, orient, slots, sends,
    v, outgoing, ghosts, hots, total, halves, from_core, along_z, along_xy, final,
    load_sem, halo_send, halo_recv, send_sem, recv_sem,
):
    layers, cells = settle.shape
    width = probes.shape[0] // layers
    halo = sends.shape[1] // 2
    me = lax.axis_index("cells")
    core, z, block = lax.rem(me, 2), lax.rem(me // 2, Z), me // (2 * Z)
    y, x = block // X, lax.rem(block, X)
    sibling = me + 1 - 2 * core
    distant = lax.rem(me + devices + 2 * core - 1, devices)
    z_peers = [me + 2 * (lax.rem(z + step, Z) - z) for step in far_first(Z)]
    xy_peers = [
        (lax.rem(y + dy, Y) * X + lax.rem(x + dx, X)) * 2 * Z + z * 2 + core
        for dy, dx in far_first(Y, X)
    ]

    loads = {}
    starts = [sum(SENT[:chunk]) for chunk in range(len(SENT))]
    spans = [pl.ds(start, size) for start, size in zip(starts, SENT)]
    plan = [("sends", sends_in, sends), ("area", area_in, area)]
    plan += [(chunk, probes_in.at[span], probes.at[span]) for chunk, span in enumerate(spans)]
    plan += [
        ("slots", slots_in, slots), ("courant", courant_in, courant),
        ("orient", orient_in, orient), ("settle", settle_in, settle),
    ]
    for index, (name, source, target) in enumerate(plan):
        loads[name] = pltpu.make_async_copy(source, target, load_sem.at[index])
        loads[name].start()

    barrier = pltpu.get_barrier_semaphore()
    greeted = [sibling, distant] + z_peers + xy_peers
    for peer in greeted:
        pl.semaphore_signal(barrier, inc=1, device_id=(peer,), device_id_type=MESH)

    one, zero = jnp.bfloat16(1), jnp.bfloat16(0)
    loads["sends"].wait()
    pick = jnp.where(
        lax.broadcasted_iota(jnp.int32, (cells, 2 * halo), 0) == sends[...], one, zero
    )
    loads["area"].wait()
    cell_area = area[...]
    inverse_area = 1.0 / cell_area
    copies = []
    for chunk, rows in enumerate(spans):
        loads[chunk].wait()
        part = (probes[rows, :].astype(jnp.float32) * inverse_area).astype(jnp.bfloat16)
        v[rows, :] = part
        picked = jnp.dot(part, pick, preferred_element_type=jnp.float32).astype(jnp.bfloat16)
        outgoing[0, rows, :] = picked[:, :halo]
        outgoing[1, rows, :] = picked[:, halo:]
        if chunk == 0:
            pl.semaphore_wait(barrier, len(greeted))
        copies.append(pltpu.make_async_remote_copy(
            src_ref=outgoing.at[core, rows, :],
            dst_ref=ghosts.at[1, rows, :],
            send_sem=halo_send.at[chunk],
            recv_sem=halo_recv.at[chunk],
            device_id=(distant,),
            device_id_type=MESH,
        ))
        copies[-1].start()
    beside = pltpu.make_async_remote_copy(
        src_ref=outgoing.at[1 - core],
        dst_ref=ghosts.at[0],
        send_sem=halo_send.at[len(SENT)],
        recv_sem=halo_recv.at[len(SENT)],
        device_id=(sibling,),
        device_id_type=MESH,
    )
    beside.start()

    for name in ("slots", "courant", "orient", "settle"):
        loads[name].wait()
    root = jnp.sqrt(cell_area)
    settled = settle[...]
    weights = [courant[face] * orient[face].astype(jnp.float32) for face in range(3)]
    keep = root * (1.0 - settled - weights[0] - weights[1] - weights[2])
    fall = root * settled
    grown = root * cell_area
    fluxes = [grown * weight for weight in weights]

    for face in range(3):
        hot = jnp.where(
            lax.broadcasted_iota(jnp.int32, (cells, cells), 0) == slots[pl.ds(face, 1), :], one, zero
        )
        for kind, side in ((0, 1 - core), (1, core)):
            place = slots[pl.ds(face, 1), :] - cells - side * halo
            hots[kind, face] = jnp.where(
                lax.broadcasted_iota(jnp.int32, (halo, cells), 0) == place, one, zero
            )
        other = jnp.dot(v[...], hot, preferred_element_type=jnp.float32)
        for layer in range(layers):
            rows = pl.ds(layer * width, width)
            term = fluxes[face][layer : layer + 1] * other[layer * width : (layer + 1) * width]
            if face == 0:
                term = term + keep[layer : layer + 1] * probes[rows, :].astype(jnp.float32)
                if layer < layers - 1:
                    lower = probes[pl.ds((layer + 1) * width, width), :]
                    term = term + fall[layer : layer + 1] * lower.astype(jnp.float32)
                total[rows, :] = term
            else:
                total[rows, :] += term

    def square_of(chunk):
        first = chunk * CHUNK // (2 * width)
        product = None
        for pair in range(first, first + CHUNK // (2 * width)):
            rows = pairs[pair]
            term = lax.dot_general(rows, rows, NT, preferred_element_type=jnp.float32)
            product = term if product is None else product + term
        return product

    beside.wait_recv()
    for face in range(3):
        other = jnp.dot(ghosts[0], hots[0, face], preferred_element_type=jnp.float32)
        for layer in range(layers):
            rows = pl.ds(layer * width, width)
            total[rows, :] += fluxes[face][layer : layer + 1] * other[layer * width : (layer + 1) * width]
    for copy in copies:
        copy.wait_recv()
    square = None
    for chunk in range(probes.shape[0] // CHUNK):
        rows = ghosts[1, pl.ds(chunk * CHUNK, CHUNK), :]
        others = [jnp.dot(rows, hots[1, face], preferred_element_type=jnp.float32) for face in range(3)]
        if chunk:
            product = square_of(chunk - 1)
            square = product if square is None else square + product
        for inner in range(CHUNK // width):
            layer = chunk * (CHUNK // width) + inner
            term = total[pl.ds(layer * width, width), :]
            for face in range(3):
                other = others[face][inner * width : (inner + 1) * width]
                term = term + fluxes[face][layer : layer + 1] * other
            high = term.astype(jnp.bfloat16)
            low = (term - high.astype(jnp.float32)).astype(jnp.bfloat16)
            pairs[layer // 2, pl.ds((layer % 2) * 2 * width, width), :] = high
            pairs[layer // 2, pl.ds((layer % 2) * 2 * width + width, width), :] = low
    square = square + square_of(probes.shape[0] // CHUNK - 1)
    w = width
    gram = None
    for layer in range(2):
        for a in range(2):
            for b in range(2):
                r, c = (2 * layer + a) * w, (2 * layer + b) * w
                piece = square[r : r + w, c : c + w]
                gram = piece if gram is None else gram + piece
    folded = jnp.concatenate([gram[: w // 2], gram[w // 2 :]], axis=1)
    halves[0] = folded[: w // 4]
    halves[1] = folded[w // 4 :]

    def send(phase, source, target, peers):
        for peer in peers:
            pltpu.make_async_remote_copy(
                src_ref=source,
                dst_ref=target,
                send_sem=send_sem.at[phase],
                recv_sem=recv_sem.at[phase],
                device_id=(peer,),
                device_id_type=MESH,
            ).start()

    def settle_all(buffer, count, semaphore):
        span = buffer.at[pl.ds(0, count)] if count else buffer
        pltpu.make_async_copy(span, span, semaphore).wait()

    def add_up(receive):
        terms = [receive[index] for index in range(receive.shape[0])]
        while len(terms) > 1:
            terms = [a + b for a, b in zip(terms[::2], terms[1::2])]
        return terms[0]

    send(0, halves.at[1 - core], from_core, [sibling])
    settle_all(from_core, 0, recv_sem.at[0])
    along_z[z] = halves[core] + from_core[...]
    send(1, along_z.at[z], along_z.at[z], z_peers)
    settle_all(along_z, Z - 1, recv_sem.at[1])
    along_xy[block] = add_up(along_z)
    send(2, along_xy.at[block], along_xy.at[block], xy_peers)
    settle_all(along_xy, X * Y - 1, recv_sem.at[2])
    final[core] = add_up(along_xy)
    send(3, final.at[core], final.at[core], [sibling])
    settle_all(from_core, 0, recv_sem.at[3])
    gram_out[...] = final[...]

    settle_all(from_core, 0, send_sem.at[0])
    settle_all(along_z, Z - 1, send_sem.at[1])
    settle_all(along_xy, X * Y - 1, send_sem.at[2])
    settle_all(from_core, 0, send_sem.at[3])
    for copy in copies + [beside]:
        copy.wait_send()


def factorize(strips, width):
    full = (8, 2 * width)
    row = lax.broadcasted_iota(jnp.int32, full, 0)
    strips = list(strips)

    def lane(values, index):
        return jnp.take_along_axis(values, jnp.full(full, index, jnp.int32), axis=1)

    def line(values, index):
        return jnp.broadcast_to(values[index : index + 1], full)

    for home in range(width // 8):
        step = 8 * home
        mine = strips[home]
        upper = [line(mine, p) for p in range(8)]
        block = [[None] * 8 for _ in range(8)]
        for q in range(8):
            column = lane(mine, step + q)
            for p in range(q + 1):
                block[p][q] = line(column, p)
        ratio = [[None] * 8 for _ in range(8)]
        scaled = []
        for p in range(8):
            reciprocal = 1.0 / block[p][p]
            for q in range(p + 1, 8):
                ratio[q][p] = block[p][q] * reciprocal
            for q in range(p + 1, 8):
                for t in range(q, 8):
                    block[q][t] = block[q][t] - ratio[q][p] * block[p][t]
                upper[q] = upper[q] - ratio[q][p] * upper[p]
            scaled.append(upper[p] * reciprocal)
        for strip in range(home + 1, width // 8):
            columns = [lane(strips[strip], step + q) for q in range(8)]
            for p in range(8):
                for q in range(p + 1, 8):
                    columns[q] = columns[q] - ratio[q][p] * columns[p]
            terms = [c * n for c, n in zip(columns, scaled)]
            while len(terms) > 1:
                terms = [a + b for a, b in zip(terms[::2], terms[1::2])]
            strips[strip] = strips[strip] - terms[0]
        done = None
        for p in range(8):
            scaled_row = upper[p] / jnp.sqrt(block[p][p])
            done = scaled_row if done is None else jnp.where(row == p, scaled_row, done)
        yield done


def basis_kernel(scale, pairs, gram, basis, factor, results, store_sem):
    groups = pairs.shape[0]
    width = factor.shape[0]
    part = width // PARTS
    folded = jnp.concatenate([gram[0], gram[1]], axis=0)
    whole = jnp.concatenate([folded[:, :width], folded[:, width:]], axis=0)
    unit = (lax.broadcasted_iota(jnp.int32, (width, width), 0)
            == lax.broadcasted_iota(jnp.int32, (width, width), 1)).astype(jnp.float32)
    work = jnp.concatenate([whole, unit], axis=1)
    finished = factorize([work[8 * i : 8 * i + 8] for i in range(width // 8)], width)
    row = lax.broadcasted_iota(jnp.int32, (part, 2 * width), 0)
    lane = lax.broadcasted_iota(jnp.int32, (part, 2 * width), 1)
    none = jnp.zeros((part, width), jnp.bfloat16)
    stores = []
    for index in range(PARTS):
        first = index * part
        rows = jnp.concatenate([next(finished) for _ in range(part // 8)], axis=0)
        factor[pl.ds(first, part), :] = jnp.where(lane >= row + first, rows, 0.0)[:, :width] / scale
        inverse = jnp.where(lane - width <= row + first, rows, 0.0)[:, width:] * scale
        high = inverse.astype(jnp.bfloat16)
        low = (inverse - high.astype(jnp.float32)).astype(jnp.bfloat16)
        stacked = jnp.concatenate([
            jnp.concatenate(blocks, axis=1)
            for value in (high, low)
            for blocks in ([value, value, none, none], [none, none, value, value])
        ], axis=0)
        for group in range(groups):
            product = jnp.dot(stacked, pairs[group], preferred_element_type=jnp.float32)
            product = product[: 2 * part] + product[2 * part :]
            for layer in range(2):
                target = pl.ds(layer * width + first, part)
                results[group, target, :] = product[layer * part : (layer + 1) * part]
                copy = pltpu.make_async_copy(
                    results.at[group, target, :], basis.at[group, target, :],
                    store_sem.at[index, 2 * group + layer],
                )
                copy.start()
                stores.append(copy)
    for copy in stores:
        copy.wait()


def body(probes, area, settle, courant, orient, local_slot, send_rows):
    layers, width, cells = probes.shape
    halo = send_rows.shape[0] // 2
    devices = lax.axis_size("cells")
    groups = layers // 2
    vmem = pl.BlockSpec(memory_space=pltpu.VMEM)
    hbm = pl.BlockSpec(memory_space=pltpu.HBM)
    sent = len(SENT)
    inputs = (
        probes.reshape(layers * width, cells), area[None, :], settle, courant, orient,
        local_slot, send_rows[None, :],
    )
    half = (width // 4, 2 * width)
    pairs, gram = pl.pallas_call(
        functools.partial(advect_kernel, devices),
        out_shape=(
            jax.ShapeDtypeStruct((groups, 4 * width, cells), jnp.bfloat16),
            jax.ShapeDtypeStruct((2, *half), jnp.float32),
        ),
        in_specs=[hbm] * 7,
        out_specs=(vmem, vmem),
        scratch_shapes=[pltpu.VMEM(array.shape, array.dtype) for array in inputs] + [
            pltpu.VMEM((layers * width, cells), jnp.bfloat16),
            pltpu.VMEM((2, layers * width, halo), jnp.bfloat16),
            pltpu.VMEM((2, layers * width, halo), jnp.bfloat16),
            pltpu.VMEM((2, 3, halo, cells), jnp.bfloat16),
            pltpu.VMEM((layers * width, cells), jnp.float32),
            pltpu.VMEM((2, *half), jnp.float32),
            pltpu.VMEM(half, jnp.float32),
            pltpu.VMEM((Z, *half), jnp.float32),
            pltpu.VMEM((X * Y, *half), jnp.float32),
            pltpu.VMEM((2, *half), jnp.float32),
            pltpu.SemaphoreType.DMA((6 + sent,)),
            pltpu.SemaphoreType.DMA((sent + 1,)),
            pltpu.SemaphoreType.DMA((sent + 1,)),
            pltpu.SemaphoreType.DMA((4,)),
            pltpu.SemaphoreType.DMA((4,)),
        ],
        compiler_params=pltpu.CompilerParams(
            collective_id=0, has_side_effects=True, vmem_limit_bytes=44 * 2**20
        ),
        name="advect",
    )(*(pltpu.with_memory_space_constraint(array, pltpu.HBM) for array in inputs))
    scale = math.sqrt(layers * cells * devices)
    basis, factor = pl.pallas_call(
        functools.partial(basis_kernel, scale),
        out_shape=(
            jax.ShapeDtypeStruct((groups, 2 * width, cells), jnp.float32),
            jax.ShapeDtypeStruct((width, width), jnp.float32),
        ),
        in_specs=[vmem, vmem],
        out_specs=(hbm, vmem),
        scratch_shapes=[
            pltpu.VMEM((groups, 2 * width, cells), jnp.float32),
            pltpu.SemaphoreType.DMA((PARTS, layers)),
        ],
        compiler_params=pltpu.CompilerParams(vmem_limit_bytes=24 * 2**20),
        name="basis",
    )(pairs, gram)
    return basis.reshape(layers, width, cells), factor


def solution(mesh):
    in_specs = (
        P(None, None, "cells"),
        P("cells"),
        P(None, "cells"),
        P(None, None, "cells"),
        P(None, None, "cells"),
        P(None, "cells"),
        P("cells"),
    )
    out_specs = (P(None, None, "cells"), P())
    return jax.shard_map(body, mesh=mesh, in_specs=in_specs, out_specs=out_specs, check_vma=False)
```

```python
import functools
import itertools
import math

import jax
import jax.numpy as jnp
from jax import lax
from jax.experimental import pallas as pl
from jax.experimental.pallas import tpu as pltpu
from jax.sharding import PartitionSpec as P

MESH = pl.DeviceIdType.MESH
Y, X, Z = 4, 4, 8
SENT = (512, 512)
CHUNKS = (256, 256, 256, 128, 128)
PARTS = 2
NT = (((1,), (1,)), ((), ()))


def far_first(*sizes):
    offsets = itertools.product(*(range(size) for size in sizes))
    away = lambda offset: sum(min(o, s - o) for o, s in zip(offset, sizes))
    ordered = sorted((o for o in offsets if any(o)), key=away, reverse=True)
    return ordered if len(sizes) > 1 else [o for o, in ordered]


def advect_kernel(
    devices, probes_in, area_in, settle_in, courant_in, orient_in, slots_in, sends_in,
    pairs, gram_out,
    probes, area, settle, courant, orient, slots, sends,
    v, outgoing, ghosts, hots, total, halves, from_core, along_z, along_xy, final,
    load_sem, halo_send, halo_recv, send_sem, recv_sem,
):
    layers, cells = settle.shape
    width = probes.shape[0] // layers
    halo = sends.shape[1] // 2
    me = lax.axis_index("cells")
    core, z, block = lax.rem(me, 2), lax.rem(me // 2, Z), me // (2 * Z)
    y, x = block // X, lax.rem(block, X)
    sibling = me + 1 - 2 * core
    distant = lax.rem(me + devices + 2 * core - 1, devices)
    z_peers = [me + 2 * (lax.rem(z + step, Z) - z) for step in far_first(Z)]
    xy_peers = [
        (lax.rem(y + dy, Y) * X + lax.rem(x + dx, X)) * 2 * Z + z * 2 + core
        for dy, dx in far_first(Y, X)
    ]

    loads = {}
    starts = [sum(SENT[:chunk]) for chunk in range(len(SENT))]
    spans = [pl.ds(start, size) for start, size in zip(starts, SENT)]
    plan = [("sends", sends_in, sends), ("area", area_in, area)]
    plan += [(chunk, probes_in.at[span], probes.at[span]) for chunk, span in enumerate(spans)]
    urgent = len(plan)
    plan += [
        ("slots", slots_in, slots), ("courant", courant_in, courant),
        ("orient", orient_in, orient), ("settle", settle_in, settle),
    ]
    for index, (name, source, target) in enumerate(plan):
        loads[name] = pltpu.make_async_copy(source, target, load_sem.at[index])
    for name, _, _ in plan[:urgent]:
        loads[name].start()

    barrier = pltpu.get_barrier_semaphore()
    greeted = [sibling, distant] + z_peers + xy_peers
    for peer in greeted:
        pl.semaphore_signal(barrier, inc=1, device_id=(peer,), device_id_type=MESH)
    for name, _, _ in plan[urgent:]:
        loads[name].start()

    one, zero = jnp.bfloat16(1), jnp.bfloat16(0)
    loads["sends"].wait()
    pick = jnp.where(
        lax.broadcasted_iota(jnp.int32, (cells, 2 * halo), 0) == sends[...], one, zero
    )
    loads["area"].wait()
    cell_area = area[...]
    inverse_area = 1.0 / cell_area
    copies = []
    for chunk, rows in enumerate(spans):
        loads[chunk].wait()
        part = (probes[rows, :].astype(jnp.float32) * inverse_area).astype(jnp.bfloat16)
        v[rows, :] = part
        picked = jnp.dot(part, pick, preferred_element_type=jnp.float32).astype(jnp.bfloat16)
        outgoing[0, rows, :] = picked[:, :halo]
        outgoing[1, rows, :] = picked[:, halo:]
        if chunk == 0:
            pl.semaphore_wait(barrier, len(greeted))
        copies.append(pltpu.make_async_remote_copy(
            src_ref=outgoing.at[core, rows, :],
            dst_ref=ghosts.at[1, rows, :],
            send_sem=halo_send.at[chunk],
            recv_sem=halo_recv.at[chunk],
            device_id=(distant,),
            device_id_type=MESH,
        ))
        copies[-1].start()
    beside = pltpu.make_async_remote_copy(
        src_ref=outgoing.at[1 - core],
        dst_ref=ghosts.at[0],
        send_sem=halo_send.at[len(SENT)],
        recv_sem=halo_recv.at[len(SENT)],
        device_id=(sibling,),
        device_id_type=MESH,
    )
    beside.start()

    for name in ("slots", "courant", "orient", "settle"):
        loads[name].wait()
    root = jnp.sqrt(cell_area)
    settled = settle[...]
    weights = [courant[face] * orient[face].astype(jnp.float32) for face in range(3)]
    keep = root * (1.0 - settled - weights[0] - weights[1] - weights[2])
    fall = root * settled
    grown = root * cell_area
    fluxes = [grown * weight for weight in weights]

    for face in range(3):
        hot = jnp.where(
            lax.broadcasted_iota(jnp.int32, (cells, cells), 0) == slots[pl.ds(face, 1), :], one, zero
        )
        for kind, side in ((0, 1 - core), (1, core)):
            place = slots[pl.ds(face, 1), :] - cells - side * halo
            hots[kind, face] = jnp.where(
                lax.broadcasted_iota(jnp.int32, (halo, cells), 0) == place, one, zero
            )
        other = jnp.dot(v[...], hot, preferred_element_type=jnp.float32)
        for layer in range(layers):
            rows = pl.ds(layer * width, width)
            term = fluxes[face][layer : layer + 1] * other[layer * width : (layer + 1) * width]
            if face == 0:
                term = term + keep[layer : layer + 1] * probes[rows, :].astype(jnp.float32)
                if layer < layers - 1:
                    lower = probes[pl.ds((layer + 1) * width, width), :]
                    term = term + fall[layer : layer + 1] * lower.astype(jnp.float32)
                total[rows, :] = term
            else:
                total[rows, :] += term

    def square_of(start, size):
        product = None
        for pair in range(start // (2 * width), (start + size) // (2 * width)):
            rows = pairs[pair]
            term = lax.dot_general(rows, rows, NT, preferred_element_type=jnp.float32)
            product = term if product is None else product + term
        return product

    beside.wait_recv()
    for face in range(3):
        other = jnp.dot(ghosts[0], hots[0, face], preferred_element_type=jnp.float32)
        for layer in range(layers):
            rows = pl.ds(layer * width, width)
            total[rows, :] += fluxes[face][layer : layer + 1] * other[layer * width : (layer + 1) * width]
    for copy in copies:
        copy.wait_recv()
    square = None
    blocks = [(sum(CHUNKS[:index]), size) for index, size in enumerate(CHUNKS)]
    for index, (start, size) in enumerate(blocks):
        rows = ghosts[1, pl.ds(start, size), :]
        others = [jnp.dot(rows, hots[1, face], preferred_element_type=jnp.float32) for face in range(3)]
        if index:
            product = square_of(*blocks[index - 1])
            square = product if square is None else square + product
        for inner in range(size // width):
            layer = start // width + inner
            term = total[pl.ds(layer * width, width), :]
            for face in range(3):
                other = others[face][inner * width : (inner + 1) * width]
                term = term + fluxes[face][layer : layer + 1] * other
            high = term.astype(jnp.bfloat16)
            low = (term - high.astype(jnp.float32)).astype(jnp.bfloat16)
            pairs[layer // 2, pl.ds((layer % 2) * 2 * width, width), :] = high
            pairs[layer // 2, pl.ds((layer % 2) * 2 * width + width, width), :] = low
    square = square + square_of(*blocks[-1])
    w = width
    gram = None
    for layer in range(2):
        for a in range(2):
            for b in range(2):
                r, c = (2 * layer + a) * w, (2 * layer + b) * w
                piece = square[r : r + w, c : c + w]
                gram = piece if gram is None else gram + piece
    folded = jnp.concatenate([gram[: w // 2], gram[w // 2 :]], axis=1)
    halves[0] = folded[: w // 4]
    halves[1] = folded[w // 4 :]

    def send(phase, source, target, peers):
        for peer in peers:
            pltpu.make_async_remote_copy(
                src_ref=source,
                dst_ref=target,
                send_sem=send_sem.at[phase],
                recv_sem=recv_sem.at[phase],
                device_id=(peer,),
                device_id_type=MESH,
            ).start()

    def settle_all(buffer, count, semaphore):
        span = buffer.at[pl.ds(0, count)] if count else buffer
        pltpu.make_async_copy(span, span, semaphore).wait()

    def add_up(receive):
        terms = [receive[index] for index in range(receive.shape[0])]
        while len(terms) > 1:
            terms = [a + b for a, b in zip(terms[::2], terms[1::2])]
        return terms[0]

    send(0, halves.at[1 - core], from_core, [sibling])
    settle_all(from_core, 0, recv_sem.at[0])
    along_z[z] = halves[core] + from_core[...]
    send(1, along_z.at[z], along_z.at[z], z_peers)
    settle_all(along_z, Z - 1, recv_sem.at[1])
    along_xy[block] = add_up(along_z)
    send(2, along_xy.at[block], along_xy.at[block], xy_peers)
    settle_all(along_xy, X * Y - 1, recv_sem.at[2])
    final[core] = add_up(along_xy)
    send(3, final.at[core], final.at[core], [sibling])
    settle_all(from_core, 0, recv_sem.at[3])
    gram_out[...] = final[...]

    settle_all(from_core, 0, send_sem.at[0])
    settle_all(along_z, Z - 1, send_sem.at[1])
    settle_all(along_xy, X * Y - 1, send_sem.at[2])
    settle_all(from_core, 0, send_sem.at[3])
    for copy in copies + [beside]:
        copy.wait_send()


def factorize(strips, width):
    full = (8, 2 * width)
    row = lax.broadcasted_iota(jnp.int32, full, 0)
    strips = list(strips)

    def lane(values, index):
        return jnp.take_along_axis(values, jnp.full(full, index, jnp.int32), axis=1)

    def line(values, index):
        return jnp.broadcast_to(values[index : index + 1], full)

    for home in range(width // 8):
        step = 8 * home
        mine = strips[home]
        upper = [line(mine, p) for p in range(8)]
        block = [[None] * 8 for _ in range(8)]
        for q in range(8):
            column = lane(mine, step + q)
            for p in range(q + 1):
                block[p][q] = line(column, p)
        ratio = [[None] * 8 for _ in range(8)]
        scaled = []
        for p in range(8):
            reciprocal = 1.0 / block[p][p]
            for q in range(p + 1, 8):
                ratio[q][p] = block[p][q] * reciprocal
            for q in range(p + 1, 8):
                for t in range(q, 8):
                    block[q][t] = block[q][t] - ratio[q][p] * block[p][t]
                upper[q] = upper[q] - ratio[q][p] * upper[p]
            scaled.append(upper[p] * reciprocal)
        for strip in range(home + 1, width // 8):
            columns = [lane(strips[strip], step + q) for q in range(8)]
            for p in range(8):
                for q in range(p + 1, 8):
                    columns[q] = columns[q] - ratio[q][p] * columns[p]
            terms = [c * n for c, n in zip(columns, scaled)]
            while len(terms) > 1:
                terms = [a + b for a, b in zip(terms[::2], terms[1::2])]
            strips[strip] = strips[strip] - terms[0]
        done = None
        for p in range(8):
            scaled_row = upper[p] / jnp.sqrt(block[p][p])
            done = scaled_row if done is None else jnp.where(row == p, scaled_row, done)
        yield done


def basis_kernel(scale, pairs, gram, basis, factor, results, store_sem):
    groups = pairs.shape[0]
    width = factor.shape[0]
    part = width // PARTS
    folded = jnp.concatenate([gram[0], gram[1]], axis=0)
    whole = jnp.concatenate([folded[:, :width], folded[:, width:]], axis=0)
    unit = (lax.broadcasted_iota(jnp.int32, (width, width), 0)
            == lax.broadcasted_iota(jnp.int32, (width, width), 1)).astype(jnp.float32)
    work = jnp.concatenate([whole, unit], axis=1)
    finished = factorize([work[8 * i : 8 * i + 8] for i in range(width // 8)], width)
    row = lax.broadcasted_iota(jnp.int32, (part, 2 * width), 0)
    lane = lax.broadcasted_iota(jnp.int32, (part, 2 * width), 1)
    none = jnp.zeros((part, width), jnp.bfloat16)
    stores = []
    for index in range(PARTS):
        first = index * part
        rows = jnp.concatenate([next(finished) for _ in range(part // 8)], axis=0)
        factor[pl.ds(first, part), :] = jnp.where(lane >= row + first, rows, 0.0)[:, :width] / scale
        inverse = jnp.where(lane - width <= row + first, rows, 0.0)[:, width:] * scale
        high = inverse.astype(jnp.bfloat16)
        low = (inverse - high.astype(jnp.float32)).astype(jnp.bfloat16)
        stacked = jnp.concatenate([
            jnp.concatenate(blocks, axis=1)
            for value in (high, low)
            for blocks in ([value, value, none, none], [none, none, value, value])
        ], axis=0)
        for group in range(groups):
            product = jnp.dot(stacked, pairs[group], preferred_element_type=jnp.float32)
            product = product[: 2 * part] + product[2 * part :]
            for layer in range(2):
                target = pl.ds(layer * width + first, part)
                results[group, target, :] = product[layer * part : (layer + 1) * part]
                copy = pltpu.make_async_copy(
                    results.at[group, target, :], basis.at[group, target, :],
                    store_sem.at[index, 2 * group + layer],
                )
                copy.start()
                stores.append(copy)
    for copy in stores:
        copy.wait()


def body(probes, area, settle, courant, orient, local_slot, send_rows):
    layers, width, cells = probes.shape
    halo = send_rows.shape[0] // 2
    devices = lax.axis_size("cells")
    groups = layers // 2
    vmem = pl.BlockSpec(memory_space=pltpu.VMEM)
    hbm = pl.BlockSpec(memory_space=pltpu.HBM)
    sent = len(SENT)
    inputs = (
        probes.reshape(layers * width, cells), area[None, :], settle, courant, orient,
        local_slot, send_rows[None, :],
    )
    half = (width // 4, 2 * width)
    pairs, gram = pl.pallas_call(
        functools.partial(advect_kernel, devices),
        out_shape=(
            jax.ShapeDtypeStruct((groups, 4 * width, cells), jnp.bfloat16),
            jax.ShapeDtypeStruct((2, *half), jnp.float32),
        ),
        in_specs=[hbm] * 7,
        out_specs=(vmem, vmem),
        scratch_shapes=[pltpu.VMEM(array.shape, array.dtype) for array in inputs] + [
            pltpu.VMEM((layers * width, cells), jnp.bfloat16),
            pltpu.VMEM((2, layers * width, halo), jnp.bfloat16),
            pltpu.VMEM((2, layers * width, halo), jnp.bfloat16),
            pltpu.VMEM((2, 3, halo, cells), jnp.bfloat16),
            pltpu.VMEM((layers * width, cells), jnp.float32),
            pltpu.VMEM((2, *half), jnp.float32),
            pltpu.VMEM(half, jnp.float32),
            pltpu.VMEM((Z, *half), jnp.float32),
            pltpu.VMEM((X * Y, *half), jnp.float32),
            pltpu.VMEM((2, *half), jnp.float32),
            pltpu.SemaphoreType.DMA((6 + sent,)),
            pltpu.SemaphoreType.DMA((sent + 1,)),
            pltpu.SemaphoreType.DMA((sent + 1,)),
            pltpu.SemaphoreType.DMA((4,)),
            pltpu.SemaphoreType.DMA((4,)),
        ],
        compiler_params=pltpu.CompilerParams(
            collective_id=0, has_side_effects=True, vmem_limit_bytes=44 * 2**20
        ),
        name="advect",
    )(*(pltpu.with_memory_space_constraint(array, pltpu.HBM) for array in inputs))
    scale = math.sqrt(layers * cells * devices)
    basis, factor = pl.pallas_call(
        functools.partial(basis_kernel, scale),
        out_shape=(
            jax.ShapeDtypeStruct((groups, 2 * width, cells), jnp.float32),
            jax.ShapeDtypeStruct((width, width), jnp.float32),
        ),
        in_specs=[vmem, vmem],
        out_specs=(hbm, vmem),
        scratch_shapes=[
            pltpu.VMEM((groups, 2 * width, cells), jnp.float32),
            pltpu.SemaphoreType.DMA((PARTS, layers)),
        ],
        compiler_params=pltpu.CompilerParams(vmem_limit_bytes=24 * 2**20),
        name="basis",
    )(pairs, gram)
    return basis.reshape(layers, width, cells), factor


def solution(mesh):
    in_specs = (
        P(None, None, "cells"),
        P("cells"),
        P(None, "cells"),
        P(None, None, "cells"),
        P(None, None, "cells"),
        P(None, "cells"),
        P("cells"),
    )
    out_specs = (P(None, None, "cells"), P())
    return jax.shard_map(body, mesh=mesh, in_specs=in_specs, out_specs=out_specs, check_vma=False)
```

```python
import functools
import itertools
import math

import jax
import jax.numpy as jnp
from jax import lax
from jax.experimental import pallas as pl
from jax.experimental.pallas import tpu as pltpu
from jax.sharding import PartitionSpec as P

MESH = pl.DeviceIdType.MESH
Y, X, Z = 4, 4, 8
SENT = (512, 512)
CHUNKS = (256, 256, 256, 128, 128)
PARTS = 2
NT = (((1,), (1,)), ((), ()))


def far_first(*sizes):
    offsets = itertools.product(*(range(size) for size in sizes))
    away = lambda offset: sum(min(o, s - o) for o, s in zip(offset, sizes))
    ordered = sorted((o for o in offsets if any(o)), key=away, reverse=True)
    return ordered if len(sizes) > 1 else [o for o, in ordered]


def advect_kernel(
    devices, probes_in, area_in, settle_in, courant_in, orient_in, slots_in, sends_in,
    pairs, gram_out,
    probes, area, settle, courant, orient, slots, sends,
    v, outgoing, ghosts, hots, total, halves, from_core, along_z, along_xy, final,
    load_sem, halo_send, halo_recv, send_sem, recv_sem,
):
    layers, cells = settle.shape
    width = probes.shape[0] // layers
    halo = sends.shape[1] // 2
    me = lax.axis_index("cells")
    core, z, block = lax.rem(me, 2), lax.rem(me // 2, Z), me // (2 * Z)
    y, x = block // X, lax.rem(block, X)
    sibling = me + 1 - 2 * core
    distant = lax.rem(me + devices + 2 * core - 1, devices)
    z_peers = [me + 2 * (lax.rem(z + step, Z) - z) for step in far_first(Z)]
    xy_peers = [
        (lax.rem(y + dy, Y) * X + lax.rem(x + dx, X)) * 2 * Z + z * 2 + core
        for dy, dx in far_first(Y, X)
    ]

    loads = {}
    starts = [sum(SENT[:chunk]) for chunk in range(len(SENT))]
    spans = [pl.ds(start, size) for start, size in zip(starts, SENT)]
    plan = [("sends", sends_in, sends), ("area", area_in, area)]
    plan += [(chunk, probes_in.at[span], probes.at[span]) for chunk, span in enumerate(spans)]
    urgent = len(plan)
    plan += [
        ("slots", slots_in, slots), ("courant", courant_in, courant),
        ("orient", orient_in, orient), ("settle", settle_in, settle),
    ]
    for index, (name, source, target) in enumerate(plan):
        loads[name] = pltpu.make_async_copy(source, target, load_sem.at[index])
    for name, _, _ in plan[:urgent]:
        loads[name].start()

    barrier = pltpu.get_barrier_semaphore()
    greeted = [sibling, distant] + z_peers + xy_peers
    for peer in greeted:
        pl.semaphore_signal(barrier, inc=1, device_id=(peer,), device_id_type=MESH)
    for name, _, _ in plan[urgent:]:
        loads[name].start()

    one, zero = jnp.bfloat16(1), jnp.bfloat16(0)
    loads["sends"].wait()
    pick = jnp.where(
        lax.broadcasted_iota(jnp.int32, (cells, 2 * halo), 0) == sends[...], one, zero
    )
    loads["area"].wait()
    cell_area = area[...]
    inverse_area = 1.0 / cell_area
    copies = []
    for chunk, rows in enumerate(spans):
        loads[chunk].wait()
        part = (probes[rows, :].astype(jnp.float32) * inverse_area).astype(jnp.bfloat16)
        v[rows, :] = part
        picked = jnp.dot(part, pick, preferred_element_type=jnp.float32).astype(jnp.bfloat16)
        outgoing[0, rows, :] = picked[:, :halo]
        outgoing[1, rows, :] = picked[:, halo:]
        if chunk == 0:
            pl.semaphore_wait(barrier, len(greeted))
        copies.append(pltpu.make_async_remote_copy(
            src_ref=outgoing.at[core, rows, :],
            dst_ref=ghosts.at[1, rows, :],
            send_sem=halo_send.at[chunk],
            recv_sem=halo_recv.at[chunk],
            device_id=(distant,),
            device_id_type=MESH,
        ))
        copies[-1].start()
    beside = pltpu.make_async_remote_copy(
        src_ref=outgoing.at[1 - core],
        dst_ref=ghosts.at[0],
        send_sem=halo_send.at[len(SENT)],
        recv_sem=halo_recv.at[len(SENT)],
        device_id=(sibling,),
        device_id_type=MESH,
    )
    beside.start()

    for name in ("slots", "courant", "orient", "settle"):
        loads[name].wait()
    root = jnp.sqrt(cell_area)
    settled = settle[...]
    weights = [courant[face] * orient[face].astype(jnp.float32) for face in range(3)]
    keep = root * (1.0 - settled - weights[0] - weights[1] - weights[2])
    fall = root * settled
    grown = root * cell_area
    fluxes = [grown * weight for weight in weights]

    for face in range(3):
        hot = jnp.where(
            lax.broadcasted_iota(jnp.int32, (cells, cells), 0) == slots[pl.ds(face, 1), :], one, zero
        )
        for kind, side in ((0, 1 - core), (1, core)):
            place = slots[pl.ds(face, 1), :] - cells - side * halo
            hots[kind, face] = jnp.where(
                lax.broadcasted_iota(jnp.int32, (halo, cells), 0) == place, one, zero
            )
        other = jnp.dot(v[...], hot, preferred_element_type=jnp.float32)
        for layer in range(layers):
            rows = pl.ds(layer * width, width)
            term = fluxes[face][layer : layer + 1] * other[layer * width : (layer + 1) * width]
            if face == 0:
                term = term + keep[layer : layer + 1] * probes[rows, :].astype(jnp.float32)
                if layer < layers - 1:
                    lower = probes[pl.ds((layer + 1) * width, width), :]
                    term = term + fall[layer : layer + 1] * lower.astype(jnp.float32)
                total[rows, :] = term
            else:
                total[rows, :] += term

    def square_of(start, size):
        product = None
        for pair in range(start // (2 * width), (start + size) // (2 * width)):
            rows = pairs[pair]
            term = lax.dot_general(rows, rows, NT, preferred_element_type=jnp.float32)
            product = term if product is None else product + term
        return product

    beside.wait_recv()
    for face in range(3):
        other = jnp.dot(ghosts[0], hots[0, face], preferred_element_type=jnp.float32)
        for layer in range(layers):
            rows = pl.ds(layer * width, width)
            total[rows, :] += fluxes[face][layer : layer + 1] * other[layer * width : (layer + 1) * width]
    for copy in copies:
        copy.wait_recv()
    square = None
    blocks = [(sum(CHUNKS[:index]), size) for index, size in enumerate(CHUNKS)]
    for index, (start, size) in enumerate(blocks):
        rows = ghosts[1, pl.ds(start, size), :]
        others = [jnp.dot(rows, hots[1, face], preferred_element_type=jnp.float32) for face in range(3)]
        if index:
            product = square_of(*blocks[index - 1])
            square = product if square is None else square + product
        for inner in range(size // width):
            layer = start // width + inner
            term = total[pl.ds(layer * width, width), :]
            for face in range(3):
                other = others[face][inner * width : (inner + 1) * width]
                term = term + fluxes[face][layer : layer + 1] * other
            high = term.astype(jnp.bfloat16)
            low = (term - high.astype(jnp.float32)).astype(jnp.bfloat16)
            pairs[layer // 2, pl.ds((layer % 2) * 2 * width, width), :] = high
            pairs[layer // 2, pl.ds((layer % 2) * 2 * width + width, width), :] = low
    square = square + square_of(*blocks[-1])
    w = width
    gram = None
    for layer in range(2):
        for a in range(2):
            for b in range(2):
                r, c = (2 * layer + a) * w, (2 * layer + b) * w
                piece = square[r : r + w, c : c + w]
                gram = piece if gram is None else gram + piece
    folded = jnp.concatenate([gram[: w // 2], gram[w // 2 :]], axis=1)
    halves[0] = folded[: w // 4]
    halves[1] = folded[w // 4 :]

    def send(phase, source, target, peers):
        for peer in peers:
            pltpu.make_async_remote_copy(
                src_ref=source,
                dst_ref=target,
                send_sem=send_sem.at[phase],
                recv_sem=recv_sem.at[phase],
                device_id=(peer,),
                device_id_type=MESH,
            ).start()

    def settle_all(buffer, count, semaphore):
        span = buffer.at[pl.ds(0, count)] if count else buffer
        pltpu.make_async_copy(span, span, semaphore).wait()

    def add_up(receive):
        terms = [receive[index] for index in range(receive.shape[0])]
        while len(terms) > 1:
            terms = [a + b for a, b in zip(terms[::2], terms[1::2])]
        return terms[0]

    send(0, halves.at[1 - core], from_core, [sibling])
    settle_all(from_core, 0, recv_sem.at[0])
    along_z[z] = halves[core] + from_core[...]
    send(1, along_z.at[z], along_z.at[z], z_peers)
    settle_all(along_z, Z - 1, recv_sem.at[1])
    along_xy[block] = add_up(along_z)
    send(2, along_xy.at[block], along_xy.at[block], xy_peers)
    settle_all(along_xy, X * Y - 1, recv_sem.at[2])
    final[core] = add_up(along_xy)
    send(3, final.at[core], final.at[core], [sibling])
    settle_all(from_core, 0, recv_sem.at[3])
    gram_out[...] = final[...]

    settle_all(from_core, 0, send_sem.at[0])
    settle_all(along_z, Z - 1, send_sem.at[1])
    settle_all(along_xy, X * Y - 1, send_sem.at[2])
    settle_all(from_core, 0, send_sem.at[3])
    for copy in copies + [beside]:
        copy.wait_send()


def factorize(strips, width):
    full = (8, 2 * width)
    row = lax.broadcasted_iota(jnp.int32, full, 0)
    strips = list(strips)

    def lane(values, index):
        return jnp.take_along_axis(values, jnp.full(full, index, jnp.int32), axis=1)

    def line(values, index):
        return jnp.broadcast_to(values[index : index + 1], full)

    for home in range(width // 8):
        step = 8 * home
        mine = strips[home]
        upper = [line(mine, p) for p in range(8)]
        block = [[None] * 8 for _ in range(8)]
        for q in range(8):
            column = lane(mine, step + q)
            for p in range(q + 1):
                block[p][q] = line(column, p)
        ratio = [[None] * 8 for _ in range(8)]
        scaled = []
        for p in range(8):
            reciprocal = 1.0 / block[p][p]
            for q in range(p + 1, 8):
                ratio[q][p] = block[p][q] * reciprocal
            for q in range(p + 1, 8):
                for t in range(q, 8):
                    block[q][t] = block[q][t] - ratio[q][p] * block[p][t]
                upper[q] = upper[q] - ratio[q][p] * upper[p]
            scaled.append(upper[p] * reciprocal)
        for strip in range(home + 1, width // 8):
            columns = [lane(strips[strip], step + q) for q in range(8)]
            for p in range(8):
                for q in range(p + 1, 8):
                    columns[q] = columns[q] - ratio[q][p] * columns[p]
            terms = [c * n for c, n in zip(columns, scaled)]
            while len(terms) > 1:
                terms = [a + b for a, b in zip(terms[::2], terms[1::2])]
            strips[strip] = strips[strip] - terms[0]
        done = None
        for p in range(8):
            scaled_row = upper[p] / jnp.sqrt(block[p][p])
            done = scaled_row if done is None else jnp.where(row == p, scaled_row, done)
        yield done


def basis_kernel(scale, pairs, gram, basis, factor, results, store_sem):
    groups = pairs.shape[0]
    width = factor.shape[0]
    part = width // PARTS
    folded = jnp.concatenate([gram[0], gram[1]], axis=0)
    whole = jnp.concatenate([folded[:, :width], folded[:, width:]], axis=0)
    unit = (lax.broadcasted_iota(jnp.int32, (width, width), 0)
            == lax.broadcasted_iota(jnp.int32, (width, width), 1)).astype(jnp.float32)
    work = jnp.concatenate([whole, unit], axis=1)
    finished = factorize([work[8 * i : 8 * i + 8] for i in range(width // 8)], width)
    row = lax.broadcasted_iota(jnp.int32, (part, 2 * width), 0)
    lane = lax.broadcasted_iota(jnp.int32, (part, 2 * width), 1)
    none = jnp.zeros((part, width), jnp.bfloat16)
    stores = []
    for index in range(PARTS):
        first = index * part
        rows = jnp.concatenate([next(finished) for _ in range(part // 8)], axis=0)
        factor[pl.ds(first, part), :] = jnp.where(lane >= row + first, rows, 0.0)[:, :width] / scale
        inverse = jnp.where(lane - width <= row + first, rows, 0.0)[:, width:] * scale
        high = inverse.astype(jnp.bfloat16)
        low = (inverse - high.astype(jnp.float32)).astype(jnp.bfloat16)
        stacked = jnp.concatenate([
            jnp.concatenate(blocks, axis=1)
            for value in (high, low)
            for blocks in ([value, value, none, none], [none, none, value, value])
        ], axis=0)
        for group in range(groups):
            product = jnp.dot(stacked, pairs[group], preferred_element_type=jnp.float32)
            product = product[: 2 * part] + product[2 * part :]
            target = pl.ds(first, part)
            for layer in range(2):
                results[group, layer, target, :] = product[layer * part : (layer + 1) * part]
            copy = pltpu.make_async_copy(
                results.at[group, :, target, :], basis.at[group, :, target, :], store_sem.at[index, group]
            )
            copy.start()
            stores.append(copy)
    for copy in stores:
        copy.wait()


def body(probes, area, settle, courant, orient, local_slot, send_rows):
    layers, width, cells = probes.shape
    halo = send_rows.shape[0] // 2
    devices = lax.axis_size("cells")
    groups = layers // 2
    vmem = pl.BlockSpec(memory_space=pltpu.VMEM)
    hbm = pl.BlockSpec(memory_space=pltpu.HBM)
    sent = len(SENT)
    inputs = (
        probes.reshape(layers * width, cells), area[None, :], settle, courant, orient,
        local_slot, send_rows[None, :],
    )
    half = (width // 4, 2 * width)
    pairs, gram = pl.pallas_call(
        functools.partial(advect_kernel, devices),
        out_shape=(
            jax.ShapeDtypeStruct((groups, 4 * width, cells), jnp.bfloat16),
            jax.ShapeDtypeStruct((2, *half), jnp.float32),
        ),
        in_specs=[hbm] * 7,
        out_specs=(vmem, vmem),
        scratch_shapes=[pltpu.VMEM(array.shape, array.dtype) for array in inputs] + [
            pltpu.VMEM((layers * width, cells), jnp.bfloat16),
            pltpu.VMEM((2, layers * width, halo), jnp.bfloat16),
            pltpu.VMEM((2, layers * width, halo), jnp.bfloat16),
            pltpu.VMEM((2, 3, halo, cells), jnp.bfloat16),
            pltpu.VMEM((layers * width, cells), jnp.float32),
            pltpu.VMEM((2, *half), jnp.float32),
            pltpu.VMEM(half, jnp.float32),
            pltpu.VMEM((Z, *half), jnp.float32),
            pltpu.VMEM((X * Y, *half), jnp.float32),
            pltpu.VMEM((2, *half), jnp.float32),
            pltpu.SemaphoreType.DMA((6 + sent,)),
            pltpu.SemaphoreType.DMA((sent + 1,)),
            pltpu.SemaphoreType.DMA((sent + 1,)),
            pltpu.SemaphoreType.DMA((4,)),
            pltpu.SemaphoreType.DMA((4,)),
        ],
        compiler_params=pltpu.CompilerParams(
            collective_id=0, has_side_effects=True, vmem_limit_bytes=44 * 2**20
        ),
        name="advect",
    )(*(pltpu.with_memory_space_constraint(array, pltpu.HBM) for array in inputs))
    scale = math.sqrt(layers * cells * devices)
    basis, factor = pl.pallas_call(
        functools.partial(basis_kernel, scale),
        out_shape=(
            jax.ShapeDtypeStruct((groups, 2, width, cells), jnp.float32),
            jax.ShapeDtypeStruct((width, width), jnp.float32),
        ),
        in_specs=[vmem, vmem],
        out_specs=(hbm, vmem),
        scratch_shapes=[
            pltpu.VMEM((groups, 2, width, cells), jnp.float32),
            pltpu.SemaphoreType.DMA((PARTS, groups)),
        ],
        compiler_params=pltpu.CompilerParams(vmem_limit_bytes=24 * 2**20),
        name="basis",
    )(pairs, gram)
    return basis.reshape(layers, width, cells), factor


def solution(mesh):
    in_specs = (
        P(None, None, "cells"),
        P("cells"),
        P(None, "cells"),
        P(None, None, "cells"),
        P(None, None, "cells"),
        P(None, "cells"),
        P("cells"),
    )
    out_specs = (P(None, None, "cells"), P())
    return jax.shard_map(body, mesh=mesh, in_specs=in_specs, out_specs=out_specs, check_vma=False)
```
